32 devices in a mesh: ctx: 16 (over z, y, x), fsdp: 2 (over core).
Axes of the slice: x: 2, y: 2, z: 4, core: 2. Of those that a mesh axis runs over, the one named last changes fastest.
Arguments:
- tokens_in: bfloat16 [2, 2048, 1536], P('fsdp', 'ctx'), may hold values from -6 to 6
- deal_table: int32 [2, 32], P('fsdp'), may hold values from 0 to 31, as said below
- cont_id: int32 [2, 2048], P('fsdp', 'ctx'), may hold values from 0 to 1, as said below
- position: int32 [2, 2048], P('fsdp', 'ctx'), may hold values from 0 to 2047, as said below
- qkv_weight: bfloat16 [1536, 2048], P(('ctx', 'fsdp')), may hold values from -0.15625 to 0.15625
- qkv_bias: bfloat16 [2048], P(('ctx', 'fsdp')), may hold values from -3 to 3
- out_weight: bfloat16 [1536, 1536], P(('ctx', 'fsdp')), may hold values from -1.75 to 1.75
- attn_gain: bfloat16 [1536], P(('ctx', 'fsdp')), may hold values from 0.5 to 1.5
- mlp_gain: bfloat16 [1536], P(('ctx', 'fsdp')), may hold values from 0.5 to 1.5
- gate_weight: bfloat16 [1536, 8960], P(('ctx', 'fsdp')), may hold values from -0.15625 to 0.15625
- up_weight: bfloat16 [1536, 8960], P(('ctx', 'fsdp')), may hold values from -0.15625 to 0.15625
- down_weight: bfloat16 [8960, 1536], P(('ctx', 'fsdp')), may hold values from -0.0625 to 0.0625
- cotangent: bfloat16 [2, 2048, 1536], P('fsdp', 'ctx'), may hold values from -6 to 6
Outputs:
- layer_out: bfloat16 [2, 2048, 1536], P('fsdp', 'ctx')
- input_grad: float32 [2, 2048, 1536], P('fsdp', 'ctx')
- qkv_weight_grad: float32 [1536, 2048], P(('ctx', 'fsdp'))
- qkv_bias_grad: float32 [1792], P(('ctx', 'fsdp'))
- value_bias_grad: float32 [256], P(('ctx', 'fsdp'))
- out_weight_grad: float32 [1536, 1536], P(('ctx', 'fsdp'))
- attn_gain_grad: float32 [1536], P(('ctx', 'fsdp'))
- mlp_gain_grad: float32 [1536], P(('ctx', 'fsdp'))
- gate_weight_grad: float32 [1536, 8960], P(('ctx', 'fsdp'))
- up_weight_grad: float32 [1536, 8960], P(('ctx', 'fsdp'))
- down_weight_grad: float32 [8960, 1536], P(('ctx', 'fsdp'))
The draws below stay inside these ranges and needn't reach their ends.
Inputs may be any that keep to these rules, and one draw needn't show every extreme that they name: `deal_table`: each set's row is a permutation of 0 to 31: entry c * 2 + b names the block of 64 consecutive tokens of the set's order (the prompt's 1024 tokens, then 1 continuations of 1024) that ctx index c holds as its block b. `cont_id`: for the token at place t of the set's order that deal_table puts at this row: 0 if t < 1024, else 1 + (t - 1024) // 1024. `position`: for the same token: t if t < 1024, else 1024 + (t - 1024) % 1024.
All inputs are finite; a program needn't handle non-finite values.
Results may differ from the reference program's by a relative error of at most 0.018.
Values may be sent and summed in bfloat16 or wider, within the bound.
No kernel may reach another device: no remote copies, remote signals or barrier semaphores. Data moves between devices by JAX's collectives and lax.ppermute only.
A program may use at most 512 MiB of HBM per device.

```python
import jax
import jax.numpy as jnp
from jax import lax

D = 1536
H = 12
KV = 2
HD = 128
FF = 8960
TOK_DEV = 128
BLOCKS_DEV = 2
CONT_LEN = 1024
HQ = 1536
QKV = 2048
BLOCK = 64
TOKENS = 2048
PROMPT = 1024
N_CTX = 16
N_FSDP = 2


def shuffle_one(subkey):
    return jax.random.permutation(subkey, BLOCKS_DEV * N_CTX)


def dealing(key):
    subkeys = jax.random.split(jax.random.fold_in(key, 17), N_FSDP)
    return jax.vmap(shuffle_one)(subkeys).astype(jnp.int32)


def place_of(key):
    dealt_blocks = dealing(key)
    block_len = TOK_DEV // BLOCKS_DEV
    row_ids = jnp.arange(TOK_DEV * N_CTX, dtype=jnp.int32)
    return jnp.take(dealt_blocks, row_ids // block_len, axis=1) * block_len + row_ids % block_len


def draw_deal_table(key, part):
    return dealing(key)


def draw_cont_id(key, part):
    place = place_of(key)
    prompt_len = TOK_DEV * N_CTX // 2
    return jnp.where(place < prompt_len, 0, 1 + (place - prompt_len) // CONT_LEN).astype(jnp.int32)


def draw_position(key, part):
    place = place_of(key)
    prompt_len = TOK_DEV * N_CTX // 2
    return jnp.where(place < prompt_len, place, prompt_len + (place - prompt_len) % CONT_LEN).astype(jnp.int32)


def levels(key, extent, pieces, low, high):
    loudness, own = 1.0, jax.random.fold_in(key, 6)
    for dim, blocks in pieces:
        draws = jnp.exp(jax.random.uniform(jax.random.fold_in(own, dim), (blocks,), jnp.float32, low / len(pieces), high / len(pieces)))
        loudness = loudness * jnp.repeat(draws, extent[dim] // blocks).reshape([-1 if axis == dim else 1 for axis in range(len(extent))])
    return loudness


def scatter_about(key, shape, deviation, bound, shards=(), held_as=jnp.bfloat16):
    values = jax.random.normal(key, shape, jnp.float32) * deviation
    if len(shards) > 0:
        values = levels(key, shape, shards, -0.22, 0.18) * values
    return jnp.clip(values, min=-bound, max=bound).astype(held_as)


def setup_inputs(seed: int = 0) -> dict:
    keys = jax.random.split(jax.random.key(seed), 14)
    return {
        "tokens_in": scatter_about(keys[0], (N_FSDP, TOKENS, D), 1.0, 6.0, ((0, 2), (1, 16))),
        "deal_table": draw_deal_table(jax.random.fold_in(keys[13], 71), 0),
        "cont_id": draw_cont_id(jax.random.fold_in(keys[13], 71), 0),
        "position": draw_position(jax.random.fold_in(keys[13], 71), 0),
        "qkv_weight": scatter_about(keys[4], (D, QKV), D ** -0.5, 0.15625, ((0, 32),)),
        "qkv_bias": scatter_about(keys[5], (QKV,), 0.5, 3.0, ((0, 32),)),
        "out_weight": scatter_about(keys[6], (HQ, D), (max(1, HQ * 16 // TOKENS)) ** -0.5, 1.75, ((0, 32),)),
        "attn_gain": jnp.clip(1.0 + 0.1 * jax.random.normal(keys[7], (D,), jnp.float32), 0.5, 1.5).astype(jnp.bfloat16),
        "mlp_gain": jnp.clip(1.0 + 0.1 * jax.random.normal(keys[8], (D,), jnp.float32), 0.5, 1.5).astype(jnp.bfloat16),
        "gate_weight": scatter_about(keys[9], (D, FF), D ** -0.5, 0.15625, ((0, 32),)),
        "up_weight": scatter_about(keys[10], (D, FF), D ** -0.5, 0.15625, ((0, 32),)),
        "down_weight": scatter_about(keys[11], (FF, D), FF ** -0.5, 0.0625, ((0, 32),)),
        "cotangent": scatter_about(keys[12], (N_FSDP, TOKENS, D), 1.0, 6.0, ((0, 2), (1, 16))),
    }


epsilon = 1e-06
rope_base = 1000000.0
neg_large = -1e+30

@jax.custom_vjp
def low(v):
    return lax.optimization_barrier(v.astype(jnp.bfloat16)).astype(jnp.float32)

@jax.custom_vjp
def low_back(v):
    return v

def low_keep(v):
    return (low(v), None)

def low_pass(kept, grad):
    return (grad,)

def back_keep(v):
    return (v, None)

def back_low(kept, grad):
    return (low(grad),)
low.defvjp(low_keep, low_pass)
low_back.defvjp(back_keep, back_low)

def matmul(operand, weights):
    return jnp.dot(operand, weights, precision=lax.Precision.HIGHEST, preferred_element_type=jnp.float32)

def rms_scale(values):
    return values * lax.rsqrt(lax.optimization_barrier(jnp.mean(values * values, axis=-1, keepdims=True)) + epsilon)

def rope_tables(position):
    half_dim = HD // 2
    frequency = jnp.exp(-jnp.log(rope_base) * (2.0 * jnp.arange(half_dim, dtype=jnp.float32) / HD))
    angles = position.astype(jnp.float32)[:, None] * frequency[None, :]
    return (jnp.concatenate([jnp.cos(angles)] * 2, axis=-1), jnp.concatenate([jnp.sin(angles)] * 2, axis=-1))

def rotate_half(values):
    half_dim = values.shape[-1] // 2
    return jnp.concatenate([-values[..., half_dim:], values[..., :half_dim]], axis=-1)

def apply_rope(values, cosine, sine_table):
    return values * cosine[:, None, :] + rotate_half(values) * sine_table[:, None, :]

def visible_pairs(query_seq, query_pos, key_seq, key_pos):
    same_seq = key_seq[None, :] == query_seq[:, None]
    seen = (key_seq[None, :] == 0) | same_seq
    return seen & (~same_seq | (key_pos[None, :] <= query_pos[:, None]))

def layer(params, hidden_in, deal_row, cont_row, pos_row):
    qkv_w, qkv_b, out_w, attn_g, mlp_g, gate_w, up_w, down_w = params
    group_size = H // KV
    score_scale = HD ** (-0.5)
    normed = low(rms_scale(hidden_in) * attn_g)
    projected = low_back(matmul(normed, qkv_w)) + qkv_b
    cosine, sine_table = rope_tables(pos_row)
    queries = low(apply_rope(projected[:, :HQ].reshape(TOKENS, H, HD), cosine, sine_table))
    keys_all = low(apply_rope(projected[:, HQ:HQ + KV * HD].reshape(TOKENS, KV, HD), cosine, sine_table))
    values_all = low(projected[:, HQ + KV * HD:].reshape(TOKENS, KV, HD))
    row_ids = jnp.arange(TOKENS, dtype=jnp.int32)
    place = deal_row[row_ids // BLOCK] * BLOCK + row_ids % BLOCK
    key_seq = jnp.where(place < PROMPT, 0, 1 + (place - PROMPT) // CONT_LEN).astype(jnp.int32)
    key_pos = jnp.where(place < PROMPT, place, PROMPT + (place - PROMPT) % CONT_LEN).astype(jnp.int32)

    def attend_block(block_in):
        query_blk, seq_blk, pos_blk = block_in
        grouped = query_blk.reshape(TOK_DEV, KV, group_size, HD)
        scores = low_back(jnp.einsum('tkgd,nkd->tkgn', grouped, keys_all, precision=lax.Precision.HIGHEST) * score_scale)
        allowed = visible_pairs(seq_blk, pos_blk, key_seq, key_pos)[:, None, None, :]
        probs = low(jax.nn.softmax(jnp.where(allowed, scores, neg_large), axis=-1))
        return jnp.einsum('tkgn,nkd->tkgd', probs, values_all, precision=lax.Precision.HIGHEST)
    blocks = TOKENS // TOK_DEV
    mixed = lax.map(jax.checkpoint(attend_block), (queries.reshape(blocks, TOK_DEV, H, HD), cont_row.reshape(blocks, TOK_DEV), pos_row.reshape(blocks, TOK_DEV)))
    attended = low(low_back(mixed.reshape(TOKENS, HQ)))
    resid = hidden_in + low_back(matmul(attended, out_w))
    normed_mlp = low(rms_scale(resid) * mlp_g)
    gate = low_back(matmul(normed_mlp, gate_w))
    upward = low_back(matmul(normed_mlp, up_w))
    hidden = low(jax.nn.silu(gate) * upward)
    return resid + low_back(matmul(hidden, down_w))

def reference(tokens_in, deal_table, cont_id, position, qkv_weight, qkv_bias, out_weight, attn_gain, mlp_gain, gate_weight, up_weight, down_weight, cotangent):
    params = (qkv_weight.astype(jnp.float32), qkv_bias.astype(jnp.float32), out_weight.astype(jnp.float32), attn_gain.astype(jnp.float32), mlp_gain.astype(jnp.float32), gate_weight.astype(jnp.float32), up_weight.astype(jnp.float32), down_weight.astype(jnp.float32))
    outputs = []
    input_grads = []
    totals = None
    for member in range(N_FSDP):

        def one_set(weights, hidden_in):
            return layer(weights, hidden_in, deal_table[member], cont_id[member], position[member])
        result, pullback = jax.vjp(one_set, params, tokens_in[member].astype(jnp.float32))
        weight_grads, hidden_grad = pullback(cotangent[member].astype(jnp.float32))
        outputs.append(result)
        input_grads.append(hidden_grad)
        totals = weight_grads if totals is None else jax.tree.map(jnp.add, totals, weight_grads)
    split_at = HQ + KV * HD
    return (jnp.stack(outputs).astype(jnp.bfloat16), jnp.stack(input_grads), totals[0], totals[1][:split_at], totals[1][split_at:], totals[2], totals[3], totals[4], totals[5], totals[6], totals[7])
```

```python
import jax
import jax.numpy as jnp
from jax import lax
from jax.sharding import PartitionSpec as P

H = 12
KV = 2
HD = 128
BLOCKS_DEV = 2
CONT_LEN = 1024


epsilon = 1e-06
rope_base = 1000000.0
neg_large = -1e30
low = jnp.bfloat16


def rms_scale(values):
    return values * lax.rsqrt(jnp.mean(values * values, axis=-1, keepdims=True) + epsilon)


def norm_back(values, gain, incoming):
    inverse = lax.rsqrt(jnp.mean(values * values, axis=-1, keepdims=True) + epsilon)
    normal = values * inverse
    gain_grad = jnp.sum(incoming * normal, axis=0)
    scaled = incoming * gain
    return (
        inverse * (scaled - normal * jnp.mean(scaled * normal, axis=-1, keepdims=True)),
        gain_grad,
    )


def rope_tables(position):
    half_dim = HD // 2
    frequency = jnp.exp(-jnp.log(rope_base) * (2.0 * jnp.arange(half_dim, dtype=jnp.float32) / HD))
    angles = position.astype(jnp.float32)[:, None] * frequency[None, :]
    return (
        jnp.concatenate([jnp.cos(angles)] * 2, axis=-1),
        jnp.concatenate([jnp.sin(angles)] * 2, axis=-1),
    )


def rotate_half(values):
    half_dim = values.shape[-1] // 2
    return jnp.concatenate([-values[..., half_dim:], values[..., :half_dim]], axis=-1)


def apply_rope(values, cosine, sine_table):
    return values * cosine[:, None, :] + rotate_half(values) * sine_table[:, None, :]


def rope_back(incoming, cosine, sine_table):
    return incoming * cosine[:, None, :] - rotate_half(incoming * sine_table[:, None, :])


def visible_pairs(query_seq, query_pos, key_seq, key_pos):
    same_seq = key_seq[None, :] == query_seq[:, None]
    seen = (key_seq[None, :] == 0) | same_seq
    return seen & (~same_seq | (key_pos[None, :] <= query_pos[:, None]))


def key_meta(deal_row, row_ids, block_len, prompt_len):
    slots = row_ids // block_len
    matches = slots[:, None] == jnp.arange(deal_row.shape[0], dtype=jnp.int32)[None, :]
    picked = jnp.sum(jnp.where(matches, deal_row[None, :], 0), axis=1)
    place = picked * block_len + row_ids % block_len
    key_seq = jnp.where(place < prompt_len, 0, 1 + (place - prompt_len) // CONT_LEN)
    key_pos = jnp.where(place < prompt_len, place, prompt_len + (place - prompt_len) % CONT_LEN)
    return (key_seq, key_pos)


def axes_of(size):
    return {16: (4, 2, 2), 64: (2, 4, 4, 2)}.get(size, (size,))


class Grid:
    def __init__(self, size):
        self.size = size
        self.axes = axes_of(size)
        self.rank = len(self.axes)
        self.strides = []
        step = size
        for extent in self.axes:
            step //= extent
            self.strides.append(step)
        index = lax.axis_index("ctx")
        self.place = [(index // s) % e for s, e in zip(self.strides, self.axes)]

    def shift(self, values, axis, by):
        stride, extent = self.strides[axis], self.axes[axis]
        pairs = []
        for i in range(self.size):
            digit = (i // stride) % extent
            pairs.append((i, i + (((digit + by) % extent) - digit) * stride))
        return lax.ppermute(values, "ctx", pairs)

    def gather_axis(self, values, axis, absolute):
        extent = self.axes[axis]
        pieces = [values]
        for _ in range(extent - 1):
            pieces.append(self.shift(pieces[-1], axis, 1))
        if not absolute:
            return jnp.concatenate(pieces, axis=axis)
        wheel = jnp.concatenate(pieces[::-1] + pieces[:0:-1], axis=axis)
        return lax.dynamic_slice_in_dim(wheel, extent - 1 - self.place[axis], extent, axis=axis)

    def scatter_axis(self, values, axis, absolute):
        extent = self.axes[axis]

        def take(back):
            if absolute:
                spot = (self.place[axis] - back + extent) % extent
                return lax.dynamic_slice_in_dim(values, spot, 1, axis=axis)
            return lax.slice_in_dim(values, back, back + 1, axis=axis)

        total = take(extent - 1)
        for back in range(extent - 2, -1, -1):
            total = take(back) + self.shift(total, axis, -1)
        return total

    def gather(self, parts, orders, absolute):
        parts = [p.reshape((1,) * self.rank + p.shape) for p in parts]
        for stage in range(max(len(o) for o in orders)):
            parts = [
                self.gather_axis(p, o[stage], absolute) if stage < len(o) else p
                for p, o in zip(parts, orders)
            ]
        return parts

    def scatter(self, parts, orders, absolute):
        for stage in range(max(len(o) for o in orders)):
            parts = [
                self.scatter_axis(p, o[::-1][stage], absolute) if stage < len(o) else p
                for p, o in zip(parts, orders)
            ]
        return [p.reshape(p.shape[self.rank :]) for p in parts]

    def source_rows(self, first, count, over):
        index = jnp.int32(0)
        for axis in range(self.rank):
            if axis in over:
                back = jnp.arange(self.axes[axis], dtype=jnp.int32)
            else:
                back = jnp.zeros((1,), jnp.int32)
            digit = (self.place[axis] - back + self.axes[axis]) % self.axes[axis]
            shape = [1] * self.rank
            shape[axis] = digit.shape[0]
            index = index + digit.reshape(shape) * self.strides[axis]
        return index[..., None], first + jnp.arange(count, dtype=jnp.int32)


def rotations(axes):
    axes = list(axes)
    return [tuple(axes[i:] + axes[:i]) for i in range(len(axes))]


def other_core(values):
    return lax.ppermute(values, "fsdp", [(0, 1), (1, 0)])


def both_cores(values, core, axis):
    other = other_core(values)
    first = jnp.where(core == 0, values, other)
    second = jnp.where(core == 0, other, values)
    return jnp.concatenate([first, second], axis=axis)


def own_core_sum(values, core, axis):
    mine = lax.dynamic_slice_in_dim(values, core, 1, axis=axis)
    theirs = lax.dynamic_slice_in_dim(values, 1 - core, 1, axis=axis)
    return mine + other_core(theirs)


def split_rows(total, shares):
    bounds = [0]
    run = 0.0
    for share in shares[:-1]:
        run += share
        bounds.append(max(bounds[-1], int(round(total * run / 16)) * 16))
    bounds.append(total)
    return bounds


def shards(
    tokens_in,
    deal_table,
    cont_id,
    position,
    qkv_weight,
    qkv_bias,
    out_weight,
    attn_gain,
    mlp_gain,
    gate_weight,
    up_weight,
    down_weight,
    cotangent,
):
    ctx_size = lax.axis_size("ctx")
    devices = 2 * ctx_size
    core = lax.axis_index("fsdp")
    grid = Grid(ctx_size)
    all_axes = tuple(range(grid.rank))
    tok_dev, width = tokens_in.shape[1], tokens_in.shape[2]
    block_len = tok_dev // BLOCKS_DEV
    prompt_len = tok_dev * ctx_size // 2
    group_size = H // KV
    score_scale = HD ** (-0.5)
    width_q = H * HD
    width_kv = KV * HD
    deal_row = deal_table[0]
    query_seq = cont_id[0]
    query_pos = position[0]
    hidden_in = tokens_in[0].astype(jnp.float32)
    rows_w = qkv_weight.shape[0]

    ff_axes = (0, 1) if grid.rank == 3 else all_axes
    far_axes = tuple(a for a in all_axes if a not in ff_axes)
    ff_size = 1
    for a in ff_axes:
        ff_size *= grid.axes[a]
    far_size = ctx_size // ff_size
    ff_total = gate_weight.shape[1]
    ff_cols = ff_total // ff_size
    members = {}
    for i in range(ctx_size):
        key = tuple((i // grid.strides[a]) % grid.axes[a] for a in far_axes)
        members.setdefault(key, []).append(i)
    groups = [members[k] for k in sorted(members)]

    orders3 = rotations(all_axes)
    if grid.rank == 3:
        orders3 = [(2, 1, 0), (1, 0, 2), (0, 2, 1)]
        token_bounds = split_rows(tok_dev, (0.25, 0.375, 0.375))
    else:
        token_bounds = split_rows(tok_dev, (1.0 / grid.rank,) * grid.rank)
    if grid.rank == 3:
        ff_orders = [(0, 1), (1, 0)]
        ff_bounds = split_rows(tok_dev, (0.625, 0.375))
    else:
        ff_orders, ff_bounds = orders3, token_bounds

    def gather_columns(weight, pieces):
        bounds = [weight.shape[1] * i // (128 * pieces) * 128 for i in range(pieces)]
        bounds.append(weight.shape[1])
        parts = [weight[:, a:b] for a, b in zip(bounds[:-1], bounds[1:])]
        orders = (orders3 * pieces)[:pieces]
        parts = grid.gather([p[None] for p in parts], orders, True)
        parts = [both_cores(p, core, grid.rank) for p in parts]
        return [p.reshape(devices * rows_w, p.shape[-1]) for p in parts]

    def scatter_columns(grad):
        pieces = grid.rank
        lead = grid.axes + (2, rows_w)
        bounds = [grad.shape[1] * i // (128 * pieces) * 128 for i in range(pieces)]
        bounds.append(grad.shape[1])
        parts = [
            own_core_sum(
                grad[:, a:b].astype(low).reshape(lead + (b - a,)), core, grid.rank
            )
            for a, b in zip(bounds[:-1], bounds[1:])
        ]
        parts = grid.scatter(parts, orders3, True)
        return jnp.concatenate([p[0] for p in parts], axis=1).astype(jnp.float32)

    def gather_tokens(values, bounds, orders):
        parts = [values[a:b] for a, b in zip(bounds[:-1], bounds[1:])]
        parts = grid.gather(parts, orders, False)
        return jnp.concatenate([p.reshape(-1, p.shape[-1]) for p in parts], axis=0)

    def scatter_tokens(values, bounds, orders, over):
        parts = []
        start = 0
        lead = tuple(grid.axes[a] if a in over else 1 for a in all_axes)
        count = 1
        for e in lead:
            count *= e
        for a, b in zip(bounds[:-1], bounds[1:]):
            rows = count * (b - a)
            parts.append(values[start : start + rows].reshape(lead + (b - a, values.shape[-1])))
            start += rows
        return jnp.concatenate(grid.scatter(parts, orders, False), axis=0)

    side_rows = jnp.zeros((rows_w, 128), low)
    bias_len = qkv_bias.shape[0]
    side_rows = side_rows.at[0, :rows_w].set(attn_gain)
    side_rows = side_rows.at[1, :rows_w].set(mlp_gain)
    side_rows = side_rows.at[2, :bias_len].set(qkv_bias)
    kv_cols, q_front, q_back = gather_columns(
        jnp.concatenate(
            [qkv_weight[:, width_q:], side_rows, qkv_weight[:, :width_q]], axis=1
        ),
        3,
    )
    full_kv_q = jnp.concatenate([kv_cols, q_front, q_back], axis=1)
    side = full_kv_q[:, 2 * width_kv : 2 * width_kv + 128].reshape(devices, rows_w, 128)
    full_attn_gain = side[:, 0, :rows_w].reshape(-1).astype(jnp.float32)
    full_mlp_gain = side[:, 1, :rows_w].reshape(-1).astype(jnp.float32)
    full_bias = side[:, 2, :bias_len].reshape(-1).astype(jnp.float32)
    full_qkv = jnp.concatenate(
        [full_kv_q[:, 2 * width_kv + 128 :], full_kv_q[:, : 2 * width_kv]], axis=1
    )
    full_out = jnp.concatenate(gather_columns(out_weight, grid.rank), axis=1)

    normed = (rms_scale(hidden_in) * full_attn_gain).astype(low)
    projected = jnp.dot(normed, full_qkv, preferred_element_type=jnp.float32) + full_bias
    cosine, sine_table = rope_tables(query_pos)
    query_low = apply_rope(
        projected[:, :width_q].reshape(tok_dev, H, HD), cosine, sine_table
    ).astype(low)
    key_low = apply_rope(
        projected[:, width_q : width_q + width_kv].reshape(tok_dev, KV, HD), cosine, sine_table
    ).astype(low)
    value_low = projected[:, width_q + width_kv :].astype(low)
    query_group = query_low.reshape(tok_dev, KV, group_size, HD)

    kv_all = gather_tokens(
        jnp.concatenate([key_low.reshape(tok_dev, width_kv), value_low], axis=1),
        token_bounds,
        orders3,
    )
    total_keys = kv_all.shape[0]
    key_all = kv_all[:, :width_kv].reshape(total_keys, KV, HD)
    value_all = kv_all[:, width_kv:].reshape(total_keys, KV, HD)
    row_ids = []
    for a, b in zip(token_bounds[:-1], token_bounds[1:]):
        chips, rows = grid.source_rows(a, b - a, all_axes)
        row_ids.append((chips * tok_dev + rows).reshape(-1))
    row_ids = jnp.concatenate(row_ids)
    key_seq, key_pos = key_meta(deal_row, row_ids, block_len, prompt_len)
    allowed = visible_pairs(query_seq, query_pos, key_seq, key_pos)[:, None, None, :]

    scores = (
        jnp.einsum("tkgd,nkd->tkgn", query_group, key_all, preferred_element_type=jnp.float32)
        * score_scale
    )
    scores = jnp.where(allowed, scores, neg_large)
    top = jnp.max(scores, axis=-1)
    weights = jnp.exp(scores - top[..., None])
    weight_sum = jnp.sum(weights, axis=-1)
    mixed = (
        jnp.einsum(
            "tkgn,nkd->tkgd", weights.astype(low), value_all, preferred_element_type=jnp.float32
        )
        / weight_sum[..., None]
    )
    log_total = top + jnp.log(weight_sum)
    attended = mixed.reshape(tok_dev, width_q).astype(low)
    resid = hidden_in + jnp.dot(attended, full_out, preferred_element_type=jnp.float32)
    normed_mlp = (rms_scale(resid) * full_mlp_gain).astype(low)

    def to_columns(weight):
        return jnp.swapaxes(weight.reshape(rows_w, ff_size, ff_cols), 0, 1)

    gate_up = jnp.concatenate([to_columns(gate_weight), to_columns(up_weight)], axis=2)
    gate_up = lax.all_to_all(
        gate_up, "ctx", split_axis=0, concat_axis=0, tiled=True, axis_index_groups=groups
    )
    lead = tuple(grid.axes[a] if a in ff_axes else 1 for a in all_axes)
    gate_up = gate_up.reshape(lead + (1, rows_w, 2 * ff_cols))
    for a in far_axes:
        gate_up = grid.gather_axis(gate_up, a, True)
    gate_up = both_cores(gate_up, core, grid.rank).reshape(width, 2 * ff_cols)
    rows_d = down_weight.shape[0]
    down = down_weight.reshape((1,) * (grid.rank + 1) + down_weight.shape)
    for a in far_axes:
        down = grid.gather_axis(down, a, True)
    down = both_cores(down, core, grid.rank).reshape(ff_cols, width)

    out_low = cotangent[0]
    out_grad = out_low.astype(jnp.float32)
    cot_all = gather_tokens(out_low, ff_bounds, ff_orders)
    mlp_all = gather_tokens(normed_mlp, ff_bounds, ff_orders)

    hidden_grad = jnp.einsum("td,fd->tf", cot_all, down, preferred_element_type=jnp.float32)
    gate_up_pre = jnp.dot(mlp_all, gate_up, preferred_element_type=jnp.float32)
    gate_pre, up_pre = gate_up_pre[:, :ff_cols], gate_up_pre[:, ff_cols:]
    sigmoid_gate = jax.nn.sigmoid(gate_pre)
    gate_act = gate_pre * sigmoid_gate
    hidden_low = (gate_act * up_pre).astype(low)
    gate_grad = (
        hidden_grad * up_pre * sigmoid_gate * (1.0 + gate_pre * (1.0 - sigmoid_gate))
    ).astype(low)
    up_grad = (hidden_grad * gate_act).astype(low)
    both_grads = jnp.concatenate([gate_grad, up_grad], axis=1)
    mlp_partial = jnp.einsum(
        "tf,df->td", both_grads, gate_up, preferred_element_type=jnp.float32
    ).astype(low)
    mlp_normed_grad = scatter_tokens(mlp_partial, ff_bounds, ff_orders, ff_axes).astype(
        jnp.float32
    )
    out_partial = jnp.dot(hidden_low, down, preferred_element_type=jnp.float32).astype(low)
    layer_out = resid + scatter_tokens(out_partial, ff_bounds, ff_orders, ff_axes).astype(
        jnp.float32
    )

    gate_up_grad = jnp.einsum("td,tf->df", mlp_all, both_grads, preferred_element_type=jnp.float32)
    gate_up_grad = gate_up_grad.astype(low).reshape(grid.axes + (2, rows_w, 2 * ff_cols))
    gate_up_grad = own_core_sum(gate_up_grad, core, grid.rank)
    for a in far_axes:
        gate_up_grad = grid.scatter_axis(gate_up_grad, a, True)
    gate_up_grad = gate_up_grad.reshape(ff_size, rows_w, 2 * ff_cols)
    gate_up_grad = lax.all_to_all(
        gate_up_grad, "ctx", split_axis=0, concat_axis=0, tiled=True, axis_index_groups=groups
    ).astype(jnp.float32)

    def to_rows(grad):
        return jnp.swapaxes(grad, 0, 1).reshape(rows_w, ff_total)

    gate_share = to_rows(gate_up_grad[:, :, :ff_cols])
    up_share = to_rows(gate_up_grad[:, :, ff_cols:])
    down_grad = jnp.einsum("tf,td->fd", hidden_low, cot_all, preferred_element_type=jnp.float32)
    far_lead = tuple(grid.axes[a] if a in far_axes else 1 for a in all_axes)
    down_grad = down_grad.astype(low).reshape(far_lead + (2, rows_d, width))
    down_grad = own_core_sum(down_grad, core, grid.rank)
    for a in far_axes:
        down_grad = grid.scatter_axis(down_grad, a, True)
    down_share = down_grad.reshape(rows_d, width).astype(jnp.float32)

    resid_part, mlp_gain_grad = norm_back(resid, full_mlp_gain, mlp_normed_grad)
    resid_grad = out_grad + resid_part
    resid_low = resid_grad.astype(low)
    out_w_grad = jnp.einsum("tq,td->qd", attended, resid_low, preferred_element_type=jnp.float32)
    out_share = scatter_columns(out_w_grad)
    mixed_grad = (
        jnp.einsum("td,qd->tq", resid_low, full_out, preferred_element_type=jnp.float32)
        .astype(low)
        .reshape(tok_dev, KV, group_size, HD)
    )
    row_dot = jnp.sum(mixed_grad.astype(jnp.float32) * mixed, axis=-1)
    scores = (
        jnp.einsum("tkgd,nkd->tkgn", query_group, key_all, preferred_element_type=jnp.float32)
        * score_scale
    )
    probs = jnp.exp(jnp.where(allowed, scores - log_total[..., None], neg_large))
    prob_grad = jnp.einsum(
        "tkgd,nkd->tkgn", mixed_grad, value_all, preferred_element_type=jnp.float32
    )
    score_grad = (probs * (prob_grad - row_dot[..., None])).astype(low)
    query_rot = (
        jnp.einsum("tkgn,nkd->tkgd", score_grad, key_all, preferred_element_type=jnp.float32)
        * score_scale
    )
    key_rot = (
        jnp.einsum("tkgn,tkgd->nkd", score_grad, query_group, preferred_element_type=jnp.float32)
        * score_scale
    )
    value_rot = jnp.einsum(
        "tkgn,tkgd->nkd", probs.astype(low), mixed_grad, preferred_element_type=jnp.float32
    )
    kv_partial = jnp.concatenate(
        [key_rot.reshape(total_keys, width_kv), value_rot.reshape(total_keys, width_kv)], axis=1
    ).astype(low)
    kv_share = scatter_tokens(kv_partial, token_bounds, orders3, all_axes).astype(jnp.float32)
    query_grad = rope_back(query_rot.reshape(tok_dev, H, HD), cosine, sine_table)
    key_grad_own = rope_back(
        kv_share[:, :width_kv].reshape(tok_dev, KV, HD), cosine, sine_table
    )
    proj_grad = jnp.concatenate(
        [
            query_grad.reshape(tok_dev, width_q),
            key_grad_own.reshape(tok_dev, width_kv),
            kv_share[:, width_kv:],
        ],
        axis=1,
    )
    bias_grad = jnp.sum(proj_grad, axis=0)
    proj_low = proj_grad.astype(low)
    qkv_w_grad = jnp.einsum("td,tc->dc", normed, proj_low, preferred_element_type=jnp.float32)
    qkv_share = scatter_columns(qkv_w_grad)
    normed_grad = jnp.einsum("tc,dc->td", proj_low, full_qkv, preferred_element_type=jnp.float32)
    input_part, attn_gain_grad = norm_back(hidden_in, full_attn_gain, normed_grad)
    input_grad = resid_grad + input_part

    small = [
        bias_grad[: width_q + width_kv],
        bias_grad[width_q + width_kv :],
        attn_gain_grad,
        mlp_gain_grad,
    ]
    small = jnp.concatenate([s.reshape(devices, -1) for s in small], axis=1)
    sizes = ((width_q + width_kv) // devices, width_kv // devices, rows_w, rows_w)
    small = jnp.pad(small, ((0, 0), (0, -small.shape[1] % 128)))
    small = jnp.sum(
        lax.all_to_all(small, ("ctx", "fsdp"), split_axis=0, concat_axis=0, tiled=True), axis=0
    )
    vectors = []
    start = 0
    for count in sizes:
        vectors.append(small[start : start + count])
        start += count
    front_share, value_bias_share, attn_gain_share, mlp_gain_share = vectors
    return (
        layer_out.astype(low)[None],
        input_grad[None],
        qkv_share,
        front_share,
        value_bias_share,
        out_share,
        attn_gain_share,
        mlp_gain_share,
        gate_share,
        up_share,
        down_share,
    )


def solution(mesh):
    return jax.shard_map(
        shards,
        mesh=mesh,
        in_specs=(
            P("fsdp", "ctx", None),
            P("fsdp", None),
            P("fsdp", "ctx"),
            P("fsdp", "ctx"),
            P(("ctx", "fsdp"), None),
            P(("ctx", "fsdp")),
            P(("ctx", "fsdp"), None),
            P(("ctx", "fsdp")),
            P(("ctx", "fsdp")),
            P(("ctx", "fsdp"), None),
            P(("ctx", "fsdp"), None),
            P(("ctx", "fsdp"), None),
            P("fsdp", "ctx", None),
        ),
        out_specs=(
            P("fsdp", "ctx", None),
            P("fsdp", "ctx", None),
            P(("ctx", "fsdp"), None),
            P(("ctx", "fsdp")),
            P(("ctx", "fsdp")),
            P(("ctx", "fsdp"), None),
            P(("ctx", "fsdp")),
            P(("ctx", "fsdp")),
            P(("ctx", "fsdp"), None),
            P(("ctx", "fsdp"), None),
            P(("ctx", "fsdp"), None),
        ),
        check_vma=False,
    )
```

```python
import itertools

import jax
import jax.numpy as jnp
from jax import lax
from jax.experimental import pallas as pl
from jax.experimental.pallas import tpu as pltpu
from jax.sharding import PartitionSpec as P

H = 12
KV = 2
HD = 128
BLOCKS_DEV = 2
CONT_LEN = 1024


epsilon = 1e-06
rope_base = 1000000.0
neg_large = -1e30
low = jnp.bfloat16


def rms_scale(values):
    return values * lax.rsqrt(jnp.mean(values * values, axis=-1, keepdims=True) + epsilon)


def norm_back(values, gain, incoming):
    inverse = lax.rsqrt(jnp.mean(values * values, axis=-1, keepdims=True) + epsilon)
    normal = values * inverse
    gain_grad = jnp.sum(incoming * normal, axis=0)
    scaled = incoming * gain
    return (
        inverse * (scaled - normal * jnp.mean(scaled * normal, axis=-1, keepdims=True)),
        gain_grad,
    )


def rope_tables(position):
    half_dim = HD // 2
    frequency = jnp.exp(-jnp.log(rope_base) * (2.0 * jnp.arange(half_dim, dtype=jnp.float32) / HD))
    angles = position.astype(jnp.float32)[:, None] * frequency[None, :]
    return (
        jnp.concatenate([jnp.cos(angles)] * 2, axis=-1),
        jnp.concatenate([jnp.sin(angles)] * 2, axis=-1),
    )


def rotate_half(values):
    half_dim = values.shape[-1] // 2
    return jnp.concatenate([-values[..., half_dim:], values[..., :half_dim]], axis=-1)


def apply_rope(values, cosine, sine_table):
    return values * cosine[:, None, :] + rotate_half(values) * sine_table[:, None, :]


def rope_back(incoming, cosine, sine_table):
    return incoming * cosine[:, None, :] - rotate_half(incoming * sine_table[:, None, :])


def visible_pairs(query_seq, query_pos, key_seq, key_pos):
    same_seq = key_seq[None, :] == query_seq[:, None]
    seen = (key_seq[None, :] == 0) | same_seq
    return seen & (~same_seq | (key_pos[None, :] <= query_pos[:, None]))


def key_meta(deal_row, row_ids, block_len, prompt_len):
    slots = row_ids // block_len
    matches = slots[:, None] == jnp.arange(deal_row.shape[0], dtype=jnp.int32)[None, :]
    picked = jnp.sum(jnp.where(matches, deal_row[None, :], 0), axis=1)
    place = picked * block_len + row_ids % block_len
    key_seq = jnp.where(place < prompt_len, 0, 1 + (place - prompt_len) // CONT_LEN)
    key_pos = jnp.where(place < prompt_len, place, prompt_len + (place - prompt_len) % CONT_LEN)
    return (key_seq, key_pos)


def axes_of(size):
    return {16: (4, 2, 2), 64: (2, 4, 4, 2)}.get(size, (size,))


def dot_nn(a, b):
    return lax.dot_general(a, b, (((1,), (0,)), ((), ())), preferred_element_type=jnp.float32)


def dot_nt(a, b):
    return lax.dot_general(a, b, (((1,), (1,)), ((), ())), preferred_element_type=jnp.float32)


def dot_tn(a, b):
    return lax.dot_general(a, b, (((0,), (0,)), ((), ())), preferred_element_type=jnp.float32)


def ff_tile(tokens, cots, gate, up, down):
    gate_pre = dot_nn(tokens, gate)
    up_pre = dot_nn(tokens, up)
    hidden_grad = dot_nt(cots, down)
    sigmoid_gate = jax.nn.sigmoid(gate_pre)
    gate_act = gate_pre * sigmoid_gate
    hidden = (gate_act * up_pre).astype(low)
    gate_grad = hidden_grad * up_pre * sigmoid_gate * (1.0 + gate_pre * (1.0 - sigmoid_gate))
    return hidden, gate_grad.astype(low), (hidden_grad * gate_act).astype(low)


def of_matrix(parts, which):
    return jnp.concatenate([p[:, which].reshape(-1, p.shape[-1]) for p in parts], axis=0)


def ff_kernel(tokens, cots, w0, w1, w2, w3, down, token_grad, out, d0, d1, d2, d3, down_grad, token_total, out_total):
    step = pl.program_id(0)
    weights = [w[...] for w in (w0, w1, w2, w3)]
    gate, up = of_matrix(weights, 0), of_matrix(weights, 1)
    hidden, gate_grad, up_grad = ff_tile(tokens[...], cots[...], gate, up, down[...])

    @pl.when(step == 0)
    def _():
        token_total[...] = jnp.zeros_like(token_total)
        out_total[...] = jnp.zeros_like(out_total)

    token_total[...] += dot_nt(gate_grad, gate) + dot_nt(up_grad, up)
    out_total[...] += dot_nn(hidden, down[...])
    for which, grad in ((0, gate_grad), (1, up_grad)):
        full = dot_tn(tokens[...], grad).astype(low)
        start = 0
        for d in (d0, d1, d2, d3):
            rows = d.shape[0] * d.shape[2]
            d[:, which] = full[start : start + rows].reshape(d.shape[0], d.shape[2], d.shape[3])
            start += rows
    down_grad[...] = dot_tn(hidden, cots[...]).astype(low)

    @pl.when(step == pl.num_programs(0) - 1)
    def _():
        token_grad[...] = token_total[...].astype(low)
        out[...] = out_total[...].astype(low)


def feed_forward(tokens, cots, weights, down):
    count, width = tokens.shape
    columns = down.shape[0]
    tile = 256
    if count > 1024 or columns % tile:
        gate, up = of_matrix(weights, 0), of_matrix(weights, 1)
        hidden, gate_grad, up_grad = ff_tile(tokens, cots, gate, up, down)
        grads = [dot_tn(tokens, g).astype(low) for g in (gate_grad, up_grad)]
        parts = []
        start = 0
        for w in weights:
            rows = w.shape[0] * w.shape[2]
            pair = [g[start : start + rows].reshape(w.shape[0], 1, *w.shape[2:]) for g in grads]
            parts.append(jnp.concatenate(pair, axis=1))
            start += rows
        return (
            (dot_nt(gate_grad, gate) + dot_nt(up_grad, up)).astype(low),
            dot_nn(hidden, down).astype(low),
            *parts,
            dot_tn(hidden, cots).astype(low),
        )
    whole = pl.BlockSpec((count, width), lambda i: (0, 0))
    pieces, _, rows, _ = weights[0].shape
    by_columns = pl.BlockSpec((pieces, 2, rows, tile), lambda i: (0, 0, 0, i))
    by_rows = pl.BlockSpec((tile, width), lambda i: (i, 0))
    wide = jax.ShapeDtypeStruct((count, width), low)
    long = jax.ShapeDtypeStruct(weights[0].shape, low)
    return pl.pallas_call(
        ff_kernel,
        grid=(columns // tile,),
        in_specs=[whole, whole] + [by_columns] * 4 + [by_rows],
        out_specs=[whole, whole] + [by_columns] * 4 + [by_rows],
        out_shape=[wide, wide] + [long] * 4 + [jax.ShapeDtypeStruct((columns, width), low)],
        scratch_shapes=[pltpu.VMEM((count, width), jnp.float32)] * 2,
        compiler_params=pltpu.CompilerParams(
            dimension_semantics=("arbitrary",), vmem_limit_bytes=50 * 1024 * 1024
        ),
        cost_estimate=pl.CostEstimate(
            flops=18 * count * width * columns,
            bytes_accessed=12 * width * columns + 12 * count * width,
            transcendentals=count * columns,
        ),
    )(tokens, cots, *weights, down)


class Grid:
    def __init__(self, size):
        self.size = size
        self.axes = axes_of(size)
        self.rank = len(self.axes)
        self.strides = []
        step = size
        for extent in self.axes:
            step //= extent
            self.strides.append(step)
        index = lax.axis_index("ctx")
        self.place = [(index // s) % e for s, e in zip(self.strides, self.axes)]

    def hop(self, values, moves):
        pairs = []
        for i in range(self.size):
            to = i
            for axis, by in moves.items():
                digit = (i // self.strides[axis]) % self.axes[axis]
                to += (((digit + by) % self.axes[axis]) - digit) * self.strides[axis]
            pairs.append((i, to))
        return lax.ppermute(values, "ctx", pairs)

    def offsets(self, axes):
        return list(itertools.product(*[range(self.axes[a]) for a in axes]))

    def gather_stage(self, values, axes):
        pieces = {}
        for offs in self.offsets(axes):
            pieces[offs] = self.hop(values, dict(zip(axes, offs))) if any(offs) else values

        def join(prefix):
            depth = len(prefix)
            if depth == len(axes):
                return pieces[prefix]
            return jnp.concatenate(
                [join(prefix + (j,)) for j in range(self.axes[axes[depth]])], axis=axes[depth]
            )

        return join(())

    def scatter_stage(self, values, axes, absolute):
        def take(offs):
            part = values
            for axis, back in zip(axes, offs):
                if absolute:
                    spot = (self.place[axis] - back + self.axes[axis]) % self.axes[axis]
                    part = lax.dynamic_slice_in_dim(part, spot, 1, axis=axis)
                else:
                    part = lax.slice_in_dim(part, back, back + 1, axis=axis)
            return part

        total = None
        arrived = []
        for offs in self.offsets(axes):
            part = take(offs)
            if any(offs):
                part = self.hop(part, {a: -o for a, o in zip(axes, offs)})
            arrived.append(part)
        total = arrived[0].astype(jnp.float32)
        for part in arrived[1:]:
            total = total + part.astype(jnp.float32)
        return total.astype(values.dtype)

    def gather(self, parts, orders):
        for stage in range(len(orders[0])):
            (parts,) = together(parts)
            parts = [self.gather_stage(p, o[stage]) for p, o in zip(parts, orders)]
        return parts

    def scatter_round(self, parts, orders, stage, absolute):
        return [
            self.scatter_stage(p, o[len(o) - 1 - stage], absolute) for p, o in zip(parts, orders)
        ]

    def ordered(self, values, axis):
        extent = self.axes[axis]
        wheel = [lax.slice_in_dim(values, j, j + 1, axis=axis) for j in range(extent)]
        wheel = jnp.concatenate(wheel[::-1] + wheel[:0:-1], axis=axis)
        return lax.dynamic_slice_in_dim(wheel, extent - 1 - self.place[axis], extent, axis=axis)

    def source_rows(self, first, count, over):
        index = jnp.int32(0)
        for axis in range(self.rank):
            if axis in over:
                back = jnp.arange(self.axes[axis], dtype=jnp.int32)
            else:
                back = jnp.zeros((1,), jnp.int32)
            digit = (self.place[axis] - back + self.axes[axis]) % self.axes[axis]
            shape = [1] * self.rank
            shape[axis] = digit.shape[0]
            index = index + digit.reshape(shape) * self.strides[axis]
        return index[..., None], first + jnp.arange(count, dtype=jnp.int32)


def together(*groups):
    flat = [v for g in groups for v in (g if isinstance(g, list) else [g])]
    flat = list(lax.optimization_barrier(tuple(flat)))
    out = []
    for g in groups:
        if isinstance(g, list):
            out.append([flat.pop(0) for _ in g])
        else:
            out.append(flat.pop(0))
    return out


def other_core(values):
    return lax.ppermute(values, "fsdp", [(0, 1), (1, 0)])


def both_cores(values, core, axis):
    other = other_core(values)
    first = jnp.where(core == 0, values, other)
    second = jnp.where(core == 0, other, values)
    return jnp.concatenate([first, second], axis=axis)


def own_core_sum(values, core, axis):
    mine = lax.dynamic_slice_in_dim(values, core, 1, axis=axis)
    theirs = lax.dynamic_slice_in_dim(values, 1 - core, 1, axis=axis)
    return mine + other_core(theirs)


def shards(
    tokens_in,
    deal_table,
    cont_id,
    position,
    qkv_weight,
    qkv_bias,
    out_weight,
    attn_gain,
    mlp_gain,
    gate_weight,
    up_weight,
    down_weight,
    cotangent,
):
    ctx_size = lax.axis_size("ctx")
    devices = 2 * ctx_size
    core = lax.axis_index("fsdp")
    grid = Grid(ctx_size)
    all_axes = tuple(range(grid.rank))
    tok_dev, width = tokens_in.shape[1], tokens_in.shape[2]
    block_len = tok_dev // BLOCKS_DEV
    prompt_len = tok_dev * ctx_size // 2
    group_size = H // KV
    score_scale = HD ** (-0.5)
    width_q = H * HD
    width_kv = KV * HD
    deal_row = deal_table[0]
    query_seq = cont_id[0]
    query_pos = position[0]
    hidden_in = tokens_in[0].astype(jnp.float32)
    rows_w = qkv_weight.shape[0]

    ff_axes = (0,) if grid.rank == 3 else all_axes
    far_axes = tuple(a for a in all_axes if a not in ff_axes)
    ff_size = 1
    for a in ff_axes:
        ff_size *= grid.axes[a]
    far_size = ctx_size // ff_size
    ff_total = gate_weight.shape[1]
    ff_cols = ff_total // ff_size
    ff_room = -(-ff_cols // 256) * 256
    members = {}
    for i in range(ctx_size):
        key = tuple((i // grid.strides[a]) % grid.axes[a] for a in far_axes)
        members.setdefault(key, []).append(i)
    groups = [members[k] for k in sorted(members)]

    if grid.rank == 3:
        wide_orders = [((0,), (1, 2))]
        ff_orders = [((0,),)]
        far_orders = [((1,), (2,)), ((2,), (1,))]
    else:
        wide_orders = [tuple((a,) for a in all_axes)]
        ff_orders = wide_orders[:1]
        far_orders = [(), ()]
    weight_order = wide_orders[:1]
    token_bounds = [0, tok_dev]
    ff_bounds = [0, tok_dev]
    far_shape = tuple(grid.axes[a] for a in far_axes)
    spots = ((core - jnp.arange(2, dtype=jnp.int32)) % 2) * rows_w
    spots = spots.reshape((2,) + (1,) * (len(far_axes) + 3))
    for slot, a in enumerate(far_axes):
        digit = (grid.place[a] - jnp.arange(grid.axes[a], dtype=jnp.int32)) % grid.axes[a]
        shape = [1] * (len(far_axes) + 4)
        shape[slot + 2] = grid.axes[a]
        spots = spots + digit.reshape(shape) * (grid.strides[a] * 2 * rows_w)
    steps = [0]
    for a in ff_axes:
        steps = [s + d * grid.strides[a] * 2 * rows_w for s in steps for d in range(grid.axes[a])]
    steps = jnp.array(steps, jnp.int32).reshape((1, 2) + (1,) * len(far_axes) + (ff_size // 2, 1))
    spots = (spots + steps + jnp.arange(rows_w, dtype=jnp.int32)).reshape(-1)
    arrival = (jnp.arange(width, dtype=jnp.int32)[:, None] == spots[None, :]).astype(low)

    def gather_tokens(values, bounds, orders):
        parts = [values[a:b] for a, b in zip(bounds[:-1], bounds[1:])]
        parts = [p.reshape((1,) * grid.rank + p.shape) for p in parts]
        parts = grid.gather(parts, orders)
        return jnp.concatenate([p.reshape(-1, p.shape[-1]) for p in parts], axis=0)

    def cut_tokens(values, bounds, over):
        parts = []
        start = 0
        lead = tuple(grid.axes[a] if a in over else 1 for a in all_axes)
        count = 1
        for e in lead:
            count *= e
        for a, b in zip(bounds[:-1], bounds[1:]):
            rows = count * (b - a)
            parts.append(values[start : start + rows].reshape(lead + (b - a, values.shape[-1])))
            start += rows
        return parts

    def join_tokens(parts):
        return jnp.concatenate([p.reshape(p.shape[grid.rank :]) for p in parts], axis=0)

    def cut_columns(grad, bounds):
        lead = grid.axes + (2, rows_w)
        return [
            own_core_sum(grad[:, a:b].astype(low).reshape(lead + (b - a,)), core, grid.rank)
            for a, b in zip(bounds[:-1], bounds[1:])
        ]

    def join_columns(parts):
        parts = [p.reshape(rows_w, p.shape[-1]) for p in parts]
        return jnp.concatenate(parts, axis=1).astype(jnp.float32)

    stages = len(wide_orders[0])
    ff_stages = len(ff_orders[0])

    bias_len = qkv_bias.shape[0]
    side_len = -(-(2 * rows_w + bias_len) // 128) * 128
    side_rows = jnp.concatenate([attn_gain, mlp_gain, qkv_bias])
    side_rows = jnp.pad(side_rows[None], ((0, rows_w - 1), (0, side_len - side_rows.shape[0])))
    gathered = lax.all_gather(
        jnp.concatenate([qkv_weight, side_rows], axis=1), ("ctx", "fsdp"), axis=0, tiled=True
    )
    def to_columns(weight):
        weight = jnp.swapaxes(weight.reshape(rows_w, ff_size, ff_cols), 0, 1)
        return jnp.pad(weight, ((0, 0), (0, 0), (0, ff_room - ff_cols)))

    gate_up = jnp.stack([to_columns(gate_weight), to_columns(up_weight)], axis=1)
    ones = (1,) * grid.rank
    rows_d = down_weight.shape[0]
    half = width // 2
    down_parts = [down_weight[:, :half].reshape(ones + (rows_d, half))]
    down_parts.append(down_weight[:, half:].reshape(ones + (rows_d, half)))
    out_low = cotangent[0]
    cot_all = gather_tokens(out_low, ff_bounds, ff_orders)

    def gather_far(parts, stage):
        if stage < len(far_orders[0]):
            parts = [grid.gather_stage(p, o[stage]) for p, o in zip(parts, far_orders)]
        return parts

    def scatter_far(parts, stage, absolute):
        if stage < len(far_orders[0]):
            parts = grid.scatter_round(parts, far_orders, stage, absolute)
        return parts

    down_parts = gather_far(down_parts, 0)
    gathered, out_weight, gate_up, cot_all, down_parts = together(
        gathered, out_weight, gate_up, cot_all, down_parts
    )
    gate_up = lax.all_to_all(
        gate_up, "ctx", split_axis=0, concat_axis=0, tiled=True, axis_index_groups=groups
    )
    few = ff_size // 2
    far_parts = [gate_up[:few], gate_up[few:]]
    far_parts = gather_far([p.reshape(ones + p.shape) for p in far_parts], 0)
    down_parts = gather_far(down_parts, 1)
    full_out = lax.all_gather(out_weight, ("ctx", "fsdp"), axis=0, tiled=True)

    full_qkv = gathered[:, : width_q + 2 * width_kv]
    side = gathered[:, width_q + 2 * width_kv :].reshape(devices, rows_w, side_len)[:, 0]
    side = side.astype(jnp.float32)
    full_attn_gain = side[:, :rows_w].reshape(-1)
    full_mlp_gain = side[:, rows_w : 2 * rows_w].reshape(-1)
    full_bias = side[:, 2 * rows_w : 2 * rows_w + bias_len].reshape(-1)

    normed = (rms_scale(hidden_in) * full_attn_gain).astype(low)
    projected = jnp.dot(normed, full_qkv, preferred_element_type=jnp.float32) + full_bias
    cosine, sine_table = rope_tables(query_pos)
    query_low = apply_rope(
        projected[:, :width_q].reshape(tok_dev, H, HD), cosine, sine_table
    ).astype(low)
    key_low = apply_rope(
        projected[:, width_q : width_q + width_kv].reshape(tok_dev, KV, HD), cosine, sine_table
    ).astype(low)
    value_low = projected[:, width_q + width_kv :].astype(low)
    query_group = query_low.reshape(tok_dev, KV, group_size, HD)

    kv_all = jnp.concatenate([key_low.reshape(tok_dev, width_kv), value_low], axis=1)
    kv_all = grid.gather_stage(kv_all.reshape(ones + kv_all.shape), wide_orders[0][0])
    kv_all, down_parts = together(kv_all, down_parts)
    for stage in range(1, len(wide_orders[0])):
        kv_all = grid.gather_stage(kv_all, wide_orders[0][stage])
    kv_all = kv_all.reshape(-1, 2 * width_kv)
    total_keys = kv_all.shape[0]
    key_all = kv_all[:, :width_kv].reshape(total_keys, KV, HD)
    value_all = kv_all[:, width_kv:].reshape(total_keys, KV, HD)
    row_ids = []
    for a, b in zip(token_bounds[:-1], token_bounds[1:]):
        chips, rows = grid.source_rows(a, b - a, all_axes)
        row_ids.append((chips * tok_dev + rows).reshape(-1))
    row_ids = jnp.concatenate(row_ids)
    key_seq, key_pos = key_meta(deal_row, row_ids, block_len, prompt_len)
    allowed = visible_pairs(query_seq, query_pos, key_seq, key_pos)[:, None, None, :]

    scores = (
        jnp.einsum("tkgd,nkd->tkgn", query_group, key_all, preferred_element_type=jnp.float32)
        * score_scale
    )
    scores = jnp.where(allowed, scores, neg_large)
    top = jnp.max(scores, axis=-1)
    weights = jnp.exp(scores - top[..., None])
    weight_sum = jnp.sum(weights, axis=-1)
    mixed = (
        jnp.einsum(
            "tkgn,nkd->tkgd", weights.astype(low), value_all, preferred_element_type=jnp.float32
        )
        / weight_sum[..., None]
    )
    log_total = top + jnp.log(weight_sum)
    attended = mixed.reshape(tok_dev, width_q).astype(low)
    resid = hidden_in + jnp.dot(attended, full_out, preferred_element_type=jnp.float32)
    normed_mlp = (rms_scale(resid) * full_mlp_gain).astype(low)

    arranged = jnp.dot(normed_mlp, arrival, preferred_element_type=jnp.float32).astype(low)
    for a in far_axes:
        down_parts = [grid.ordered(p, a) for p in down_parts]
    down = jnp.concatenate([p[..., None, :, :] for p in down_parts], axis=-1)
    down = both_cores(down, core, grid.rank).reshape(ff_cols, width)
    down = jnp.pad(down, ((0, ff_room - ff_cols), (0, 0)))
    arranged, far_parts, down = together(arranged, far_parts, down)
    mlp_all = gather_tokens(arranged, ff_bounds, ff_orders)
    far_parts = gather_far(far_parts, 1)
    mlp_all, far_parts = together(mlp_all, far_parts)
    far_parts = [p.reshape((-1,) + p.shape[-3:]) for p in far_parts]
    far_parts = far_parts + [other_core(p) for p in far_parts]

    out_grad = out_low.astype(jnp.float32)
    mlp_partial, out_partial, *far_grads, down_grad = feed_forward(
        mlp_all, cot_all, far_parts, down
    )
    far_lead = tuple(grid.axes[a] if a in far_axes else 1 for a in all_axes)
    far_grads = [
        (ours.astype(jnp.float32) + other_core(theirs).astype(jnp.float32)).astype(low)
        for ours, theirs in zip(far_grads[:2], far_grads[2:])
    ]
    far_grads = [g.reshape(far_lead + (few,) + g.shape[1:]) for g in far_grads]
    lead = tuple(grid.axes[a] if a in ff_axes else 1 for a in all_axes)
    out_partial = out_partial.reshape(lead + (tok_dev, width))
    for a in ff_axes:
        out_partial = grid.ordered(out_partial, a)
    down_grad = down_grad[:ff_cols].reshape(far_lead + (2, rows_d, width))
    down_grad = own_core_sum(down_grad, core, grid.rank)
    down_grads = [down_grad[..., :half], down_grad[..., half:]]
    mlp_partial, far_grads, down_grads = together(mlp_partial, far_grads, down_grads)
    mlp_parts = cut_tokens(mlp_partial, ff_bounds, ff_axes)
    for stage in range(ff_stages):
        mlp_parts = grid.scatter_round(mlp_parts, ff_orders, stage, False)
    far_grads = scatter_far(far_grads, 0, False)
    mlp_parts, far_grads, out_partial = together(mlp_parts, far_grads, out_partial)
    out_sum = lax.psum_scatter(
        out_partial.reshape(-1, width),
        "ctx",
        scatter_dimension=0,
        tiled=True,
        axis_index_groups=groups,
    )
    mlp_normed_grad = jnp.einsum(
        "tc,dc->td", join_tokens(mlp_parts), arrival, preferred_element_type=jnp.float32
    )
    resid_part, mlp_gain_grad = norm_back(resid, full_mlp_gain, mlp_normed_grad)
    resid_grad = out_grad + resid_part
    resid_low = resid_grad.astype(low)
    out_w_grad = jnp.einsum("tq,td->qd", attended, resid_low, preferred_element_type=jnp.float32)
    out_w_sum = lax.psum_scatter(
        out_w_grad.astype(low), ("ctx", "fsdp"), scatter_dimension=0, tiled=True
    )
    mixed_grad = (
        jnp.einsum("td,qd->tq", resid_low, full_out, preferred_element_type=jnp.float32)
        .astype(low)
        .reshape(tok_dev, KV, group_size, HD)
    )
    row_dot = jnp.sum(mixed_grad.astype(jnp.float32) * mixed, axis=-1)
    scores = (
        jnp.einsum("tkgd,nkd->tkgn", query_group, key_all, preferred_element_type=jnp.float32)
        * score_scale
    )
    probs = jnp.exp(jnp.where(allowed, scores - log_total[..., None], neg_large))
    prob_grad = jnp.einsum(
        "tkgd,nkd->tkgn", mixed_grad, value_all, preferred_element_type=jnp.float32
    )
    score_grad = (probs * (prob_grad - row_dot[..., None])).astype(low)
    query_rot = (
        jnp.einsum("tkgn,nkd->tkgd", score_grad, key_all, preferred_element_type=jnp.float32)
        * score_scale
    )
    key_rot = (
        jnp.einsum("tkgn,tkgd->nkd", score_grad, query_group, preferred_element_type=jnp.float32)
        * score_scale
    )
    value_rot = jnp.einsum(
        "tkgn,tkgd->nkd", probs.astype(low), mixed_grad, preferred_element_type=jnp.float32
    )
    kv_partial = jnp.concatenate(
        [key_rot.reshape(total_keys, width_kv), value_rot.reshape(total_keys, width_kv)], axis=1
    ).astype(low)
    query_grad = rope_back(query_rot.reshape(tok_dev, H, HD), cosine, sine_table)
    query_grad = query_grad.reshape(tok_dev, width_q)
    query_parts = cut_columns(
        jnp.einsum("td,tc->dc", normed, query_grad.astype(low), preferred_element_type=jnp.float32),
        (0, width_q),
    )

    kv_parts = cut_tokens(kv_partial, token_bounds, all_axes)
    kv_parts = grid.scatter_round(kv_parts, wide_orders, 0, False)
    kv_parts, far_grads, query_parts, down_grads = together(
        kv_parts, far_grads, query_parts, down_grads
    )
    for stage in range(1, stages):
        kv_parts = grid.scatter_round(kv_parts, wide_orders, stage, False)
    far_grads = scatter_far(far_grads, 1, False)
    kv_share = join_tokens(kv_parts).astype(jnp.float32)
    kv_share, query_parts, far_grads, down_grads = together(
        kv_share, query_parts, far_grads, down_grads
    )
    gate_up_grad = jnp.concatenate([g.reshape((few,) + g.shape[-3:]) for g in far_grads], axis=0)
    gate_up_grad = lax.all_to_all(
        gate_up_grad, "ctx", split_axis=0, concat_axis=0, tiled=True, axis_index_groups=groups
    )
    query_parts = grid.scatter_round(query_parts, weight_order, 0, True)
    down_grads = scatter_far(down_grads, 0, True)
    key_grad_own = rope_back(
        kv_share[:, :width_kv].reshape(tok_dev, KV, HD), cosine, sine_table
    )
    kv_grad = jnp.concatenate(
        [key_grad_own.reshape(tok_dev, width_kv), kv_share[:, width_kv:]], axis=1
    )
    proj_grad = jnp.concatenate([query_grad, kv_grad], axis=1)
    bias_grad = jnp.sum(proj_grad, axis=0)
    proj_low = proj_grad.astype(low)
    normed_grad = jnp.einsum("tc,dc->td", proj_low, full_qkv, preferred_element_type=jnp.float32)
    input_part, attn_gain_grad = norm_back(hidden_in, full_attn_gain, normed_grad)
    input_grad = resid_grad + input_part

    input_grad, out_sum, out_w_sum = together(input_grad, out_sum, out_w_sum)
    out_share = out_w_sum.astype(jnp.float32)
    layer_out = resid + out_sum.astype(jnp.float32)

    def to_rows(grad):
        return jnp.swapaxes(grad, 0, 1).reshape(rows_w, ff_total)

    small = [
        bias_grad[: width_q + width_kv],
        bias_grad[width_q + width_kv :],
        attn_gain_grad,
        mlp_gain_grad,
    ]
    small = jnp.concatenate([v.reshape(devices, 1, -1) for v in small], axis=2).astype(low)
    sizes = ((width_q + width_kv) // devices, width_kv // devices, rows_w, rows_w)
    small = jnp.pad(small, ((0, 0), (0, rows_w - 1), (0, -small.shape[2] % 128)))
    kv_w_grad = jnp.einsum(
        "td,tc->dc", normed, kv_grad.astype(low), preferred_element_type=jnp.float32
    ).astype(low)
    kv_w_grad = jnp.concatenate([kv_w_grad, small.reshape(width, -1)], axis=1)
    kv_w_parts = cut_columns(kv_w_grad, (0, kv_w_grad.shape[1]))
    query_parts, kv_w_parts, down_grads = together(query_parts, kv_w_parts, down_grads)
    down_grads = scatter_far(down_grads, 1, True)
    down_grad = jnp.concatenate(down_grads, axis=-1)
    down_share = down_grad.reshape(rows_d, width).astype(jnp.float32)
    for stage in range(1, stages):
        query_parts = grid.scatter_round(query_parts, weight_order, stage, True)
    for stage in range(stages):
        kv_w_parts = grid.scatter_round(kv_w_parts, weight_order, stage, True)
    kv_w_share = join_columns(kv_w_parts)
    small = kv_w_share[0, 2 * width_kv :]
    qkv_share = jnp.concatenate([join_columns(query_parts), kv_w_share[:, : 2 * width_kv]], axis=1)
    gate_up_grad = gate_up_grad.astype(jnp.float32)
    gate_share = to_rows(gate_up_grad[:, 0, :, :ff_cols])
    up_share = to_rows(gate_up_grad[:, 1, :, :ff_cols])
    vectors = []
    start = 0
    for count in sizes:
        vectors.append(small[start : start + count])
        start += count
    front_share, value_bias_share, attn_gain_share, mlp_gain_share = vectors
    return (
        layer_out.astype(low)[None],
        input_grad[None],
        qkv_share,
        front_share,
        value_bias_share,
        out_share,
        attn_gain_share,
        mlp_gain_share,
        gate_share,
        up_share,
        down_share,
    )


def solution(mesh):
    return jax.shard_map(
        shards,
        mesh=mesh,
        in_specs=(
            P("fsdp", "ctx", None),
            P("fsdp", None),
            P("fsdp", "ctx"),
            P("fsdp", "ctx"),
            P(("ctx", "fsdp"), None),
            P(("ctx", "fsdp")),
            P(("ctx", "fsdp"), None),
            P(("ctx", "fsdp")),
            P(("ctx", "fsdp")),
            P(("ctx", "fsdp"), None),
            P(("ctx", "fsdp"), None),
            P(("ctx", "fsdp"), None),
            P("fsdp", "ctx", None),
        ),
        out_specs=(
            P("fsdp", "ctx", None),
            P("fsdp", "ctx", None),
            P(("ctx", "fsdp"), None),
            P(("ctx", "fsdp")),
            P(("ctx", "fsdp")),
            P(("ctx", "fsdp"), None),
            P(("ctx", "fsdp")),
            P(("ctx", "fsdp")),
            P(("ctx", "fsdp"), None),
            P(("ctx", "fsdp"), None),
            P(("ctx", "fsdp"), None),
        ),
        check_vma=False,
    )
```

```python
import itertools

import jax
import jax.numpy as jnp
from jax import lax
from jax.experimental import pallas as pl
from jax.experimental.pallas import tpu as pltpu
from jax.sharding import PartitionSpec as P

H = 12
KV = 2
HD = 128
BLOCKS_DEV = 2
CONT_LEN = 1024


epsilon = 1e-06
rope_base = 1000000.0
neg_large = -1e30
low = jnp.bfloat16


def rms_scale(values):
    return values * lax.rsqrt(jnp.mean(values * values, axis=-1, keepdims=True) + epsilon)


def norm_back(values, gain, incoming):
    inverse = lax.rsqrt(jnp.mean(values * values, axis=-1, keepdims=True) + epsilon)
    normal = values * inverse
    gain_grad = jnp.sum(incoming * normal, axis=0)
    scaled = incoming * gain
    return (
        inverse * (scaled - normal * jnp.mean(scaled * normal, axis=-1, keepdims=True)),
        gain_grad,
    )


def rope_tables(position):
    half_dim = HD // 2
    frequency = jnp.exp(-jnp.log(rope_base) * (2.0 * jnp.arange(half_dim, dtype=jnp.float32) / HD))
    angles = position.astype(jnp.float32)[:, None] * frequency[None, :]
    return (
        jnp.concatenate([jnp.cos(angles)] * 2, axis=-1),
        jnp.concatenate([jnp.sin(angles)] * 2, axis=-1),
    )


def rotate_half(values):
    half_dim = values.shape[-1] // 2
    return jnp.concatenate([-values[..., half_dim:], values[..., :half_dim]], axis=-1)


def apply_rope(values, cosine, sine_table):
    return values * cosine[:, None, :] + rotate_half(values) * sine_table[:, None, :]


def rope_back(incoming, cosine, sine_table):
    return incoming * cosine[:, None, :] - rotate_half(incoming * sine_table[:, None, :])


def visible_pairs(query_seq, query_pos, key_seq, key_pos):
    same_seq = key_seq[None, :] == query_seq[:, None]
    seen = (key_seq[None, :] == 0) | same_seq
    return seen & (~same_seq | (key_pos[None, :] <= query_pos[:, None]))


def key_meta(deal_row, row_ids, block_len, prompt_len):
    slots = row_ids // block_len
    matches = slots[:, None] == jnp.arange(deal_row.shape[0], dtype=jnp.int32)[None, :]
    picked = jnp.sum(jnp.where(matches, deal_row[None, :], 0), axis=1)
    place = picked * block_len + row_ids % block_len
    key_seq = jnp.where(place < prompt_len, 0, 1 + (place - prompt_len) // CONT_LEN)
    key_pos = jnp.where(place < prompt_len, place, prompt_len + (place - prompt_len) % CONT_LEN)
    return (key_seq, key_pos)


def axes_of(size):
    return {16: (4, 2, 2), 64: (2, 4, 4, 2)}.get(size, (size,))


def dot_nn(a, b):
    return lax.dot_general(a, b, (((1,), (0,)), ((), ())), preferred_element_type=jnp.float32)


def dot_nt(a, b):
    return lax.dot_general(a, b, (((1,), (1,)), ((), ())), preferred_element_type=jnp.float32)


def dot_tn(a, b):
    return lax.dot_general(a, b, (((0,), (0,)), ((), ())), preferred_element_type=jnp.float32)


def side_by_side(values, first, count):
    return jnp.concatenate(
        [values[:, (first + h) * HD : (first + h + 1) * HD] for h in range(count)], axis=0
    )


def attend_kernel(queries, keys_values, hidden_by, mixed, attended, log_total):
    group_size = H // KV
    tokens = queries.shape[0]
    for g in range(KV):
        query = side_by_side(queries[...], g * group_size, group_size)
        keys = keys_values[:, g * HD : (g + 1) * HD]
        values = keys_values[:, (KV + g) * HD : (KV + g + 1) * HD]
        scores = dot_nt(keys, query) * HD ** (-0.5)
        scores = scores + jnp.concatenate([hidden_by[...]] * group_size, axis=1)
        top = jnp.max(scores, axis=0, keepdims=True)
        weights = jnp.exp(scores - top)
        total = jnp.sum(weights, axis=0, keepdims=True)
        result = dot_tn(values, weights.astype(low)) / total
        log_total[g : g + 1, :] = top + jnp.log(total)
        for h in range(group_size):
            turned = result[:, h * tokens : (h + 1) * tokens].T
            spot = slice((g * group_size + h) * HD, (g * group_size + h + 1) * HD)
            mixed[:, spot] = turned
            attended[:, spot] = turned.astype(low)


def attend(queries, keys_values, hidden_by):
    tokens, width = queries.shape
    columns = H // KV * tokens
    pairs = keys_values.shape[0] * H * tokens
    return pl.pallas_call(
        attend_kernel,
        out_shape=[
            jax.ShapeDtypeStruct((tokens, width), jnp.float32),
            jax.ShapeDtypeStruct((tokens, width), low),
            jax.ShapeDtypeStruct((KV, columns), jnp.float32),
        ],
        compiler_params=pltpu.CompilerParams(vmem_limit_bytes=50 * 1024 * 1024),
        cost_estimate=pl.CostEstimate(
            flops=4 * pairs * HD, bytes_accessed=2 * keys_values.size, transcendentals=pairs
        ),
    )(queries, keys_values, hidden_by)


def attend_back_kernel(queries, keys_values, hidden_by, mixed, log_total, mixed_grad, query_grad, kv_grad):
    group_size = H // KV
    tokens = queries.shape[0]
    total_keys = keys_values.shape[0]
    chunk = min(total_keys, 512)
    scale = HD ** (-0.5)
    for g in range(KV):
        query = side_by_side(queries[...], g * group_size, group_size)
        incoming = side_by_side(mixed_grad[...], g * group_size, group_size)
        rows = []
        for h in range(group_size):
            spot = slice((g * group_size + h) * HD, (g * group_size + h + 1) * HD)
            product = mixed_grad[:, spot].astype(jnp.float32) * mixed[:, spot]
            rows.append(jnp.sum(product.T, axis=0, keepdims=True))
        row_dot = jnp.concatenate(rows, axis=1)
        turned_grad = jnp.zeros((HD, group_size * tokens), jnp.float32)
        for start in range(0, total_keys, chunk):
            part = slice(start, start + chunk)
            keys = keys_values[part, g * HD : (g + 1) * HD]
            values = keys_values[part, (KV + g) * HD : (KV + g + 1) * HD]
            scores = dot_nt(keys, query) * scale
            scores = scores + jnp.concatenate([hidden_by[part, :]] * group_size, axis=1)
            probs = jnp.exp(scores - log_total[g : g + 1, :])
            score_grad = (probs * (dot_nt(values, incoming) - row_dot)).astype(low)
            kv_grad[part, g * HD : (g + 1) * HD] = (dot_nn(score_grad, query) * scale).astype(low)
            kv_grad[part, (KV + g) * HD : (KV + g + 1) * HD] = dot_nn(
                probs.astype(low), incoming
            ).astype(low)
            turned_grad += dot_tn(keys, score_grad)
        for h in range(group_size):
            spot = slice((g * group_size + h) * HD, (g * group_size + h + 1) * HD)
            query_grad[:, spot] = turned_grad[:, h * tokens : (h + 1) * tokens].T * scale


def attend_back(queries, keys_values, hidden_by, mixed, log_total, mixed_grad):
    tokens, width = queries.shape
    pairs = keys_values.shape[0] * H * tokens
    return pl.pallas_call(
        attend_back_kernel,
        out_shape=[
            jax.ShapeDtypeStruct((tokens, width), jnp.float32),
            jax.ShapeDtypeStruct(keys_values.shape, low),
        ],
        compiler_params=pltpu.CompilerParams(vmem_limit_bytes=50 * 1024 * 1024),
        cost_estimate=pl.CostEstimate(
            flops=10 * pairs * HD, bytes_accessed=4 * keys_values.size, transcendentals=pairs
        ),
    )(queries, keys_values, hidden_by, mixed, log_total, mixed_grad)


def ff_tile(tokens, cots, gate, up, down):
    gate_pre = dot_nn(tokens, gate)
    up_pre = dot_nn(tokens, up)
    hidden_grad = dot_nt(cots, down)
    sigmoid_gate = jax.nn.sigmoid(gate_pre)
    gate_act = gate_pre * sigmoid_gate
    hidden = (gate_act * up_pre).astype(low)
    gate_grad = hidden_grad * up_pre * sigmoid_gate * (1.0 + gate_pre * (1.0 - sigmoid_gate))
    return hidden, gate_grad.astype(low), (hidden_grad * gate_act).astype(low)


def of_matrix(parts, which):
    return jnp.concatenate([p[:, which].reshape(-1, p.shape[-1]) for p in parts], axis=0)


def ff_kernel(tokens, cots, w0, w1, w2, w3, down, token_grad, out, d0, d1, d2, d3, down_grad, token_total, out_total):
    step = pl.program_id(0)
    weights = [w[...] for w in (w0, w1, w2, w3)]
    gate, up = of_matrix(weights, 0), of_matrix(weights, 1)
    hidden, gate_grad, up_grad = ff_tile(tokens[...], cots[...], gate, up, down[...])

    @pl.when(step == 0)
    def _():
        token_total[...] = jnp.zeros_like(token_total)
        out_total[...] = jnp.zeros_like(out_total)

    token_total[...] += dot_nt(gate_grad, gate) + dot_nt(up_grad, up)
    out_total[...] += dot_nn(hidden, down[...])
    for which, grad in ((0, gate_grad), (1, up_grad)):
        full = dot_tn(tokens[...], grad).astype(low)
        start = 0
        for d in (d0, d1, d2, d3):
            rows = d.shape[0] * d.shape[2]
            d[:, which] = full[start : start + rows].reshape(d.shape[0], d.shape[2], d.shape[3])
            start += rows
    down_grad[...] = dot_tn(hidden, cots[...]).astype(low)

    @pl.when(step == pl.num_programs(0) - 1)
    def _():
        token_grad[...] = token_total[...].astype(low)
        out[...] = out_total[...].astype(low)


def feed_forward(tokens, cots, weights, down):
    count, width = tokens.shape
    columns = down.shape[0]
    tile = 256
    if count > 1024 or columns % tile:
        gate, up = of_matrix(weights, 0), of_matrix(weights, 1)
        hidden, gate_grad, up_grad = ff_tile(tokens, cots, gate, up, down)
        grads = [dot_tn(tokens, g).astype(low) for g in (gate_grad, up_grad)]
        parts = []
        start = 0
        for w in weights:
            rows = w.shape[0] * w.shape[2]
            pair = [g[start : start + rows].reshape(w.shape[0], 1, *w.shape[2:]) for g in grads]
            parts.append(jnp.concatenate(pair, axis=1))
            start += rows
        return (
            (dot_nt(gate_grad, gate) + dot_nt(up_grad, up)).astype(low),
            dot_nn(hidden, down).astype(low),
            *parts,
            dot_tn(hidden, cots).astype(low),
        )
    whole = pl.BlockSpec((count, width), lambda i: (0, 0))
    pieces, _, rows, _ = weights[0].shape
    by_columns = pl.BlockSpec((pieces, 2, rows, tile), lambda i: (0, 0, 0, i))
    by_rows = pl.BlockSpec((tile, width), lambda i: (i, 0))
    wide = jax.ShapeDtypeStruct((count, width), low)
    long = jax.ShapeDtypeStruct(weights[0].shape, low)
    return pl.pallas_call(
        ff_kernel,
        grid=(columns // tile,),
        in_specs=[whole, whole] + [by_columns] * 4 + [by_rows],
        out_specs=[whole, whole] + [by_columns] * 4 + [by_rows],
        out_shape=[wide, wide] + [long] * 4 + [jax.ShapeDtypeStruct((columns, width), low)],
        scratch_shapes=[pltpu.VMEM((count, width), jnp.float32)] * 2,
        compiler_params=pltpu.CompilerParams(
            dimension_semantics=("arbitrary",), vmem_limit_bytes=50 * 1024 * 1024
        ),
        cost_estimate=pl.CostEstimate(
            flops=18 * count * width * columns,
            bytes_accessed=12 * width * columns + 12 * count * width,
            transcendentals=count * columns,
        ),
    )(tokens, cots, *weights, down)


class Grid:
    def __init__(self, size):
        self.size = size
        self.axes = axes_of(size)
        self.rank = len(self.axes)
        self.strides = []
        step = size
        for extent in self.axes:
            step //= extent
            self.strides.append(step)
        index = lax.axis_index("ctx")
        self.place = [(index // s) % e for s, e in zip(self.strides, self.axes)]

    def hop(self, values, moves):
        pairs = []
        for i in range(self.size):
            to = i
            for axis, by in moves.items():
                digit = (i // self.strides[axis]) % self.axes[axis]
                to += (((digit + by) % self.axes[axis]) - digit) * self.strides[axis]
            pairs.append((i, to))
        return lax.ppermute(values, "ctx", pairs)

    def offsets(self, axes):
        return list(itertools.product(*[range(self.axes[a]) for a in axes]))

    def gather_stage(self, values, axes):
        pieces = {}
        for offs in self.offsets(axes):
            pieces[offs] = self.hop(values, dict(zip(axes, offs))) if any(offs) else values

        def join(prefix):
            depth = len(prefix)
            if depth == len(axes):
                return pieces[prefix]
            return jnp.concatenate(
                [join(prefix + (j,)) for j in range(self.axes[axes[depth]])], axis=axes[depth]
            )

        return join(())

    def scatter_stage(self, values, axes, absolute):
        def take(offs):
            part = values
            for axis, back in zip(axes, offs):
                if absolute:
                    spot = (self.place[axis] - back + self.axes[axis]) % self.axes[axis]
                    part = lax.dynamic_slice_in_dim(part, spot, 1, axis=axis)
                else:
                    part = lax.slice_in_dim(part, back, back + 1, axis=axis)
            return part

        total = None
        arrived = []
        for offs in self.offsets(axes):
            part = take(offs)
            if any(offs):
                part = self.hop(part, {a: -o for a, o in zip(axes, offs)})
            arrived.append(part)
        total = arrived[0].astype(jnp.float32)
        for part in arrived[1:]:
            total = total + part.astype(jnp.float32)
        return total.astype(values.dtype)

    def gather(self, parts, orders):
        for stage in range(len(orders[0])):
            (parts,) = together(parts)
            parts = [self.gather_stage(p, o[stage]) for p, o in zip(parts, orders)]
        return parts

    def scatter_round(self, parts, orders, stage, absolute):
        return [
            self.scatter_stage(p, o[len(o) - 1 - stage], absolute) for p, o in zip(parts, orders)
        ]

    def ordered(self, values, axis):
        extent = self.axes[axis]
        wheel = [lax.slice_in_dim(values, j, j + 1, axis=axis) for j in range(extent)]
        wheel = jnp.concatenate(wheel[::-1] + wheel[:0:-1], axis=axis)
        return lax.dynamic_slice_in_dim(wheel, extent - 1 - self.place[axis], extent, axis=axis)

    def source_rows(self, first, count, over):
        index = jnp.int32(0)
        for axis in range(self.rank):
            if axis in over:
                back = jnp.arange(self.axes[axis], dtype=jnp.int32)
            else:
                back = jnp.zeros((1,), jnp.int32)
            digit = (self.place[axis] - back + self.axes[axis]) % self.axes[axis]
            shape = [1] * self.rank
            shape[axis] = digit.shape[0]
            index = index + digit.reshape(shape) * self.strides[axis]
        return index[..., None], first + jnp.arange(count, dtype=jnp.int32)


def together(*groups):
    flat = [v for g in groups for v in (g if isinstance(g, list) else [g])]
    flat = list(lax.optimization_barrier(tuple(flat)))
    out = []
    for g in groups:
        if isinstance(g, list):
            out.append([flat.pop(0) for _ in g])
        else:
            out.append(flat.pop(0))
    return out


def other_core(values):
    return lax.ppermute(values, "fsdp", [(0, 1), (1, 0)])


def both_cores(values, core, axis):
    other = other_core(values)
    first = jnp.where(core == 0, values, other)
    second = jnp.where(core == 0, other, values)
    return jnp.concatenate([first, second], axis=axis)


def own_core_sum(values, core, axis):
    mine = lax.dynamic_slice_in_dim(values, core, 1, axis=axis)
    theirs = lax.dynamic_slice_in_dim(values, 1 - core, 1, axis=axis)
    return mine + other_core(theirs)


def shards(
    tokens_in,
    deal_table,
    cont_id,
    position,
    qkv_weight,
    qkv_bias,
    out_weight,
    attn_gain,
    mlp_gain,
    gate_weight,
    up_weight,
    down_weight,
    cotangent,
):
    ctx_size = lax.axis_size("ctx")
    devices = 2 * ctx_size
    core = lax.axis_index("fsdp")
    grid = Grid(ctx_size)
    all_axes = tuple(range(grid.rank))
    tok_dev, width = tokens_in.shape[1], tokens_in.shape[2]
    block_len = tok_dev // BLOCKS_DEV
    prompt_len = tok_dev * ctx_size // 2
    width_q = H * HD
    width_kv = KV * HD
    deal_row = deal_table[0]
    query_seq = cont_id[0]
    query_pos = position[0]
    hidden_in = tokens_in[0].astype(jnp.float32)
    rows_w = qkv_weight.shape[0]

    ff_axes = (0,) if grid.rank == 3 else all_axes
    far_axes = tuple(a for a in all_axes if a not in ff_axes)
    ff_size = 1
    for a in ff_axes:
        ff_size *= grid.axes[a]
    far_size = ctx_size // ff_size
    ff_total = gate_weight.shape[1]
    ff_cols = ff_total // ff_size
    ff_room = -(-ff_cols // 256) * 256
    members = {}
    for i in range(ctx_size):
        key = tuple((i // grid.strides[a]) % grid.axes[a] for a in far_axes)
        members.setdefault(key, []).append(i)
    groups = [members[k] for k in sorted(members)]

    if grid.rank == 3:
        wide_orders = [((0,), (1, 2))]
        ff_orders = [((0,),)]
        far_orders = [((1,), (2,)), ((2,), (1,))]
    else:
        wide_orders = [tuple((a,) for a in all_axes)]
        ff_orders = wide_orders[:1]
        far_orders = [(), ()]
    weight_order = wide_orders[:1]
    token_bounds = [0, tok_dev]
    ff_bounds = [0, tok_dev]
    far_shape = tuple(grid.axes[a] for a in far_axes)
    spots = ((core - jnp.arange(2, dtype=jnp.int32)) % 2) * rows_w
    spots = spots.reshape((2,) + (1,) * (len(far_axes) + 3))
    for slot, a in enumerate(far_axes):
        digit = (grid.place[a] - jnp.arange(grid.axes[a], dtype=jnp.int32)) % grid.axes[a]
        shape = [1] * (len(far_axes) + 4)
        shape[slot + 2] = grid.axes[a]
        spots = spots + digit.reshape(shape) * (grid.strides[a] * 2 * rows_w)
    steps = [0]
    for a in ff_axes:
        steps = [s + d * grid.strides[a] * 2 * rows_w for s in steps for d in range(grid.axes[a])]
    steps = jnp.array(steps, jnp.int32).reshape((1, 2) + (1,) * len(far_axes) + (ff_size // 2, 1))
    spots = (spots + steps + jnp.arange(rows_w, dtype=jnp.int32)).reshape(-1)
    arrival = (jnp.arange(width, dtype=jnp.int32)[:, None] == spots[None, :]).astype(low)

    def gather_tokens(values, bounds, orders):
        parts = [values[a:b] for a, b in zip(bounds[:-1], bounds[1:])]
        parts = [p.reshape((1,) * grid.rank + p.shape) for p in parts]
        parts = grid.gather(parts, orders)
        return jnp.concatenate([p.reshape(-1, p.shape[-1]) for p in parts], axis=0)

    def cut_tokens(values, bounds, over):
        parts = []
        start = 0
        lead = tuple(grid.axes[a] if a in over else 1 for a in all_axes)
        count = 1
        for e in lead:
            count *= e
        for a, b in zip(bounds[:-1], bounds[1:]):
            rows = count * (b - a)
            parts.append(values[start : start + rows].reshape(lead + (b - a, values.shape[-1])))
            start += rows
        return parts

    def join_tokens(parts):
        return jnp.concatenate([p.reshape(p.shape[grid.rank :]) for p in parts], axis=0)

    def cut_columns(grad, bounds):
        lead = grid.axes + (2, rows_w)
        return [
            own_core_sum(grad[:, a:b].astype(low).reshape(lead + (b - a,)), core, grid.rank)
            for a, b in zip(bounds[:-1], bounds[1:])
        ]

    def join_columns(parts):
        parts = [p.reshape(rows_w, p.shape[-1]) for p in parts]
        return jnp.concatenate(parts, axis=1).astype(jnp.float32)

    stages = len(wide_orders[0])
    ff_stages = len(ff_orders[0])

    bias_len = qkv_bias.shape[0]
    side_len = -(-(2 * rows_w + bias_len) // 128) * 128
    side_rows = jnp.concatenate([attn_gain, mlp_gain, qkv_bias])
    side_rows = jnp.pad(side_rows[None], ((0, rows_w - 1), (0, side_len - side_rows.shape[0])))
    gathered = lax.all_gather(
        jnp.concatenate([qkv_weight, side_rows], axis=1), ("ctx", "fsdp"), axis=0, tiled=True
    )
    def to_columns(weight):
        weight = jnp.swapaxes(weight.reshape(rows_w, ff_size, ff_cols), 0, 1)
        return jnp.pad(weight, ((0, 0), (0, 0), (0, ff_room - ff_cols)))

    gate_up = jnp.stack([to_columns(gate_weight), to_columns(up_weight)], axis=1)
    ones = (1,) * grid.rank
    rows_d = down_weight.shape[0]
    half = width // 2
    down_parts = [down_weight[:, :half].reshape(ones + (rows_d, half))]
    down_parts.append(down_weight[:, half:].reshape(ones + (rows_d, half)))
    out_low = cotangent[0]
    cot_all = gather_tokens(out_low, ff_bounds, ff_orders)

    def gather_far(parts, stage):
        if stage < len(far_orders[0]):
            parts = [grid.gather_stage(p, o[stage]) for p, o in zip(parts, far_orders)]
        return parts

    def scatter_far(parts, stage, absolute):
        if stage < len(far_orders[0]):
            parts = grid.scatter_round(parts, far_orders, stage, absolute)
        return parts

    down_parts = gather_far(down_parts, 0)
    cot_all, down_parts = together(cot_all, down_parts)
    down_parts = gather_far(down_parts, 1)
    for a in far_axes:
        down_parts = [grid.ordered(p, a) for p in down_parts]
    down = jnp.concatenate([p[..., None, :, :] for p in down_parts], axis=-1)
    down = both_cores(down, core, grid.rank).reshape(ff_cols, width)
    down = jnp.pad(down, ((0, ff_room - ff_cols), (0, 0)))
    gathered, out_weight, gate_up, cot_all, down = together(
        gathered, out_weight, gate_up, cot_all, down
    )
    full_out = lax.all_gather(out_weight, ("ctx", "fsdp"), axis=0, tiled=True)

    full_qkv = gathered[:, : width_q + 2 * width_kv]
    side = gathered[:, width_q + 2 * width_kv :].reshape(devices, rows_w, side_len)[:, 0]
    side = side.astype(jnp.float32)
    full_attn_gain = side[:, :rows_w].reshape(-1)
    full_mlp_gain = side[:, rows_w : 2 * rows_w].reshape(-1)
    full_bias = side[:, 2 * rows_w : 2 * rows_w + bias_len].reshape(-1)

    normed = (rms_scale(hidden_in) * full_attn_gain).astype(low)
    projected = jnp.dot(normed, full_qkv, preferred_element_type=jnp.float32) + full_bias
    cosine, sine_table = rope_tables(query_pos)
    query_low = apply_rope(
        projected[:, :width_q].reshape(tok_dev, H, HD), cosine, sine_table
    ).astype(low)
    key_low = apply_rope(
        projected[:, width_q : width_q + width_kv].reshape(tok_dev, KV, HD), cosine, sine_table
    ).astype(low)
    value_low = projected[:, width_q + width_kv :].astype(low)
    query_low = query_low.reshape(tok_dev, width_q)

    kv_all = jnp.concatenate([key_low.reshape(tok_dev, width_kv), value_low], axis=1)
    kv_all = grid.gather_stage(kv_all.reshape(ones + kv_all.shape), wide_orders[0][0])
    kv_all, gate_up = together(kv_all, gate_up)
    gate_up = lax.all_to_all(
        gate_up, "ctx", split_axis=0, concat_axis=0, tiled=True, axis_index_groups=groups
    )
    for stage in range(1, len(wide_orders[0])):
        kv_all = grid.gather_stage(kv_all, wide_orders[0][stage])
    kv_all = kv_all.reshape(-1, 2 * width_kv)
    row_ids = []
    for a, b in zip(token_bounds[:-1], token_bounds[1:]):
        chips, rows = grid.source_rows(a, b - a, all_axes)
        row_ids.append((chips * tok_dev + rows).reshape(-1))
    row_ids = jnp.concatenate(row_ids)
    key_seq, key_pos = key_meta(deal_row, row_ids, block_len, prompt_len)
    allowed = visible_pairs(query_seq, query_pos, key_seq, key_pos).T
    hidden_by = jnp.where(allowed, 0.0, neg_large).astype(jnp.float32)
    mixed, attended, log_total = attend(query_low, kv_all, hidden_by)
    attended, gate_up = together(attended, gate_up)
    few = ff_size // 2
    far_parts = [gate_up[:few], gate_up[few:]]
    far_parts = gather_far([p.reshape(ones + p.shape) for p in far_parts], 0)
    resid = hidden_in + jnp.dot(attended, full_out, preferred_element_type=jnp.float32)
    normed_mlp = (rms_scale(resid) * full_mlp_gain).astype(low)

    arranged = jnp.dot(normed_mlp, arrival, preferred_element_type=jnp.float32).astype(low)
    arranged, far_parts = together(arranged, far_parts)
    mlp_all = gather_tokens(arranged, ff_bounds, ff_orders)
    far_parts = gather_far(far_parts, 1)
    mlp_all, far_parts = together(mlp_all, far_parts)
    far_parts = [p.reshape((-1,) + p.shape[-3:]) for p in far_parts]
    far_parts = far_parts + [other_core(p) for p in far_parts]

    out_grad = out_low.astype(jnp.float32)
    mlp_partial, out_partial, *far_grads, down_grad = feed_forward(
        mlp_all, cot_all, far_parts, down
    )
    far_lead = tuple(grid.axes[a] if a in far_axes else 1 for a in all_axes)
    far_grads = [
        (ours.astype(jnp.float32) + other_core(theirs).astype(jnp.float32)).astype(low)
        for ours, theirs in zip(far_grads[:2], far_grads[2:])
    ]
    far_grads = [g.reshape(far_lead + (few,) + g.shape[1:]) for g in far_grads]
    lead = tuple(grid.axes[a] if a in ff_axes else 1 for a in all_axes)
    out_partial = out_partial.reshape(lead + (tok_dev, width))
    for a in ff_axes:
        out_partial = grid.ordered(out_partial, a)
    down_grad = down_grad[:ff_cols].reshape(far_lead + (2, rows_d, width))
    down_grad = own_core_sum(down_grad, core, grid.rank)
    down_grads = [down_grad[..., :half], down_grad[..., half:]]
    mlp_partial, far_grads = together(mlp_partial, far_grads)
    mlp_parts = cut_tokens(mlp_partial, ff_bounds, ff_axes)
    for stage in range(ff_stages):
        mlp_parts = grid.scatter_round(mlp_parts, ff_orders, stage, False)
    far_grads = scatter_far(far_grads, 0, False)
    mlp_parts, far_grads, out_partial, down_grads = together(
        mlp_parts, far_grads, out_partial, down_grads
    )
    out_sum = lax.psum_scatter(
        out_partial.reshape(-1, width),
        "ctx",
        scatter_dimension=0,
        tiled=True,
        axis_index_groups=groups,
    )
    mlp_normed_grad = jnp.einsum(
        "tc,dc->td", join_tokens(mlp_parts), arrival, preferred_element_type=jnp.float32
    )
    resid_part, mlp_gain_grad = norm_back(resid, full_mlp_gain, mlp_normed_grad)
    resid_grad = out_grad + resid_part
    resid_low = resid_grad.astype(low)
    out_w_grad = jnp.einsum("tq,td->qd", attended, resid_low, preferred_element_type=jnp.float32)
    out_w_grad, resid_low = together(out_w_grad.astype(low), resid_low)
    out_w_sum = lax.psum_scatter(
        out_w_grad, ("ctx", "fsdp"), scatter_dimension=0, tiled=True
    )
    mixed_grad = jnp.einsum(
        "td,qd->tq", resid_low, full_out, preferred_element_type=jnp.float32
    ).astype(low)
    query_rot, kv_partial = attend_back(
        query_low, kv_all, hidden_by, mixed, log_total, mixed_grad
    )
    query_grad = rope_back(query_rot.reshape(tok_dev, H, HD), cosine, sine_table)
    query_grad = query_grad.reshape(tok_dev, width_q)
    query_parts = cut_columns(
        jnp.einsum("td,tc->dc", normed, query_grad.astype(low), preferred_element_type=jnp.float32),
        (0, width_q),
    )

    kv_parts = cut_tokens(kv_partial, token_bounds, all_axes)
    kv_parts = grid.scatter_round(kv_parts, wide_orders, 0, False)
    kv_parts, far_grads, query_parts, down_grads = together(
        kv_parts, far_grads, query_parts, down_grads
    )
    for stage in range(1, stages):
        kv_parts = grid.scatter_round(kv_parts, wide_orders, stage, False)
    far_grads = scatter_far(far_grads, 1, False)
    kv_share = join_tokens(kv_parts).astype(jnp.float32)
    kv_share, query_parts, far_grads, down_grads = together(
        kv_share, query_parts, far_grads, down_grads
    )
    gate_up_grad = jnp.concatenate([g.reshape((few,) + g.shape[-3:]) for g in far_grads], axis=0)
    gate_up_grad = lax.all_to_all(
        gate_up_grad, "ctx", split_axis=0, concat_axis=0, tiled=True, axis_index_groups=groups
    )
    query_parts = grid.scatter_round(query_parts, weight_order, 0, True)
    down_grads = scatter_far(down_grads, 0, True)
    key_grad_own = rope_back(
        kv_share[:, :width_kv].reshape(tok_dev, KV, HD), cosine, sine_table
    )
    kv_grad = jnp.concatenate(
        [key_grad_own.reshape(tok_dev, width_kv), kv_share[:, width_kv:]], axis=1
    )
    proj_grad = jnp.concatenate([query_grad, kv_grad], axis=1)
    bias_grad = jnp.sum(proj_grad, axis=0)
    proj_low = proj_grad.astype(low)
    normed_grad = jnp.einsum("tc,dc->td", proj_low, full_qkv, preferred_element_type=jnp.float32)
    input_part, attn_gain_grad = norm_back(hidden_in, full_attn_gain, normed_grad)
    input_grad = resid_grad + input_part

    input_grad, out_sum, out_w_sum = together(input_grad, out_sum, out_w_sum)
    out_share = out_w_sum.astype(jnp.float32)
    layer_out = resid + out_sum.astype(jnp.float32)

    def to_rows(grad):
        return jnp.swapaxes(grad, 0, 1).reshape(rows_w, ff_total)

    small = [
        bias_grad[: width_q + width_kv],
        bias_grad[width_q + width_kv :],
        attn_gain_grad,
        mlp_gain_grad,
    ]
    small = jnp.concatenate([v.reshape(devices, 1, -1) for v in small], axis=2).astype(low)
    sizes = ((width_q + width_kv) // devices, width_kv // devices, rows_w, rows_w)
    small = jnp.pad(small, ((0, 0), (0, rows_w - 1), (0, -small.shape[2] % 128)))
    kv_w_grad = jnp.einsum(
        "td,tc->dc", normed, kv_grad.astype(low), preferred_element_type=jnp.float32
    ).astype(low)
    kv_w_grad = jnp.concatenate([kv_w_grad, small.reshape(width, -1)], axis=1)
    kv_w_parts = cut_columns(kv_w_grad, (0, kv_w_grad.shape[1]))
    query_parts, kv_w_parts, down_grads = together(query_parts, kv_w_parts, down_grads)
    down_grads = scatter_far(down_grads, 1, True)
    down_grad = jnp.concatenate(down_grads, axis=-1)
    down_share = down_grad.reshape(rows_d, width).astype(jnp.float32)
    for stage in range(1, stages):
        query_parts = grid.scatter_round(query_parts, weight_order, stage, True)
    for stage in range(stages):
        kv_w_parts = grid.scatter_round(kv_w_parts, weight_order, stage, True)
    kv_w_share = join_columns(kv_w_parts)
    small = kv_w_share[0, 2 * width_kv :]
    qkv_share = jnp.concatenate([join_columns(query_parts), kv_w_share[:, : 2 * width_kv]], axis=1)
    gate_up_grad = gate_up_grad.astype(jnp.float32)
    gate_share = to_rows(gate_up_grad[:, 0, :, :ff_cols])
    up_share = to_rows(gate_up_grad[:, 1, :, :ff_cols])
    vectors = []
    start = 0
    for count in sizes:
        vectors.append(small[start : start + count])
        start += count
    front_share, value_bias_share, attn_gain_share, mlp_gain_share = vectors
    return (
        layer_out.astype(low)[None],
        input_grad[None],
        qkv_share,
        front_share,
        value_bias_share,
        out_share,
        attn_gain_share,
        mlp_gain_share,
        gate_share,
        up_share,
        down_share,
    )


def solution(mesh):
    return jax.shard_map(
        shards,
        mesh=mesh,
        in_specs=(
            P("fsdp", "ctx", None),
            P("fsdp", None),
            P("fsdp", "ctx"),
            P("fsdp", "ctx"),
            P(("ctx", "fsdp"), None),
            P(("ctx", "fsdp")),
            P(("ctx", "fsdp"), None),
            P(("ctx", "fsdp")),
            P(("ctx", "fsdp")),
            P(("ctx", "fsdp"), None),
            P(("ctx", "fsdp"), None),
            P(("ctx", "fsdp"), None),
            P("fsdp", "ctx", None),
        ),
        out_specs=(
            P("fsdp", "ctx", None),
            P("fsdp", "ctx", None),
            P(("ctx", "fsdp"), None),
            P(("ctx", "fsdp")),
            P(("ctx", "fsdp")),
            P(("ctx", "fsdp"), None),
            P(("ctx", "fsdp")),
            P(("ctx", "fsdp")),
            P(("ctx", "fsdp"), None),
            P(("ctx", "fsdp"), None),
            P(("ctx", "fsdp"), None),
        ),
        check_vma=False,
    )
```

```python
import itertools

import jax
import jax.numpy as jnp
from jax import lax
from jax.experimental import pallas as pl
from jax.experimental.pallas import tpu as pltpu
from jax.sharding import PartitionSpec as P

H = 12
KV = 2
HD = 128
BLOCKS_DEV = 2
CONT_LEN = 1024


epsilon = 1e-06
rope_base = 1000000.0
neg_large = -1e30
low = jnp.bfloat16


def rms_scale(values):
    return values * lax.rsqrt(jnp.mean(values * values, axis=-1, keepdims=True) + epsilon)


def norm_back(values, gain, incoming):
    inverse = lax.rsqrt(jnp.mean(values * values, axis=-1, keepdims=True) + epsilon)
    normal = values * inverse
    gain_grad = jnp.sum(incoming * normal, axis=0)
    scaled = incoming * gain
    return (
        inverse * (scaled - normal * jnp.mean(scaled * normal, axis=-1, keepdims=True)),
        gain_grad,
    )


def rope_tables(position):
    half_dim = HD // 2
    frequency = jnp.exp(-jnp.log(rope_base) * (2.0 * jnp.arange(half_dim, dtype=jnp.float32) / HD))
    angles = position.astype(jnp.float32)[:, None] * frequency[None, :]
    return (
        jnp.concatenate([jnp.cos(angles)] * 2, axis=-1),
        jnp.concatenate([jnp.sin(angles)] * 2, axis=-1),
    )


def rotate_half(values):
    half_dim = values.shape[-1] // 2
    return jnp.concatenate([-values[..., half_dim:], values[..., :half_dim]], axis=-1)


def apply_rope(values, cosine, sine_table):
    return values * cosine[:, None, :] + rotate_half(values) * sine_table[:, None, :]


def rope_back(incoming, cosine, sine_table):
    return incoming * cosine[:, None, :] - rotate_half(incoming * sine_table[:, None, :])


def visible_pairs(query_seq, query_pos, key_seq, key_pos):
    same_seq = key_seq[None, :] == query_seq[:, None]
    seen = (key_seq[None, :] == 0) | same_seq
    return seen & (~same_seq | (key_pos[None, :] <= query_pos[:, None]))


def key_meta(deal_row, row_ids, block_len, prompt_len):
    slots = row_ids // block_len
    matches = slots[:, None] == jnp.arange(deal_row.shape[0], dtype=jnp.int32)[None, :]
    picked = jnp.sum(jnp.where(matches, deal_row[None, :], 0), axis=1)
    place = picked * block_len + row_ids % block_len
    key_seq = jnp.where(place < prompt_len, 0, 1 + (place - prompt_len) // CONT_LEN)
    key_pos = jnp.where(place < prompt_len, place, prompt_len + (place - prompt_len) % CONT_LEN)
    return (key_seq, key_pos)


def axes_of(size):
    return {16: (4, 2, 2), 64: (2, 4, 4, 2)}.get(size, (size,))


def dot_nn(a, b):
    return lax.dot_general(a, b, (((1,), (0,)), ((), ())), preferred_element_type=jnp.float32)


def dot_nt(a, b):
    return lax.dot_general(a, b, (((1,), (1,)), ((), ())), preferred_element_type=jnp.float32)


def dot_tn(a, b):
    return lax.dot_general(a, b, (((0,), (0,)), ((), ())), preferred_element_type=jnp.float32)


def side_by_side(values, first, count):
    return jnp.concatenate(
        [values[:, (first + h) * HD : (first + h + 1) * HD] for h in range(count)], axis=0
    )


def attend_kernel(queries, keys_values, hidden_by, mixed, attended, log_total):
    group_size = H // KV
    tokens = queries.shape[0]
    for g in range(KV):
        query = side_by_side(queries[...], g * group_size, group_size)
        keys = keys_values[:, g * HD : (g + 1) * HD]
        values = keys_values[:, (KV + g) * HD : (KV + g + 1) * HD]
        scores = dot_nt(keys, query) * HD ** (-0.5)
        scores = scores + jnp.concatenate([hidden_by[...]] * group_size, axis=1)
        top = jnp.max(scores, axis=0, keepdims=True)
        weights = jnp.exp(scores - top)
        total = jnp.sum(weights, axis=0, keepdims=True)
        result = dot_tn(values, weights.astype(low)) / total
        log_total[g : g + 1, :] = top + jnp.log(total)
        for h in range(group_size):
            turned = result[:, h * tokens : (h + 1) * tokens].T
            spot = slice((g * group_size + h) * HD, (g * group_size + h + 1) * HD)
            mixed[:, spot] = turned
            attended[:, spot] = turned.astype(low)


def attend(queries, keys_values, hidden_by):
    tokens, width = queries.shape
    columns = H // KV * tokens
    pairs = keys_values.shape[0] * H * tokens
    return pl.pallas_call(
        attend_kernel,
        out_shape=[
            jax.ShapeDtypeStruct((tokens, width), jnp.float32),
            jax.ShapeDtypeStruct((tokens, width), low),
            jax.ShapeDtypeStruct((KV, columns), jnp.float32),
        ],
        compiler_params=pltpu.CompilerParams(vmem_limit_bytes=50 * 1024 * 1024),
        cost_estimate=pl.CostEstimate(
            flops=4 * pairs * HD, bytes_accessed=2 * keys_values.size, transcendentals=pairs
        ),
    )(queries, keys_values, hidden_by)


def attend_back_kernel(queries, keys_values, hidden_by, mixed, log_total, mixed_grad, query_grad, kv_grad):
    group_size = H // KV
    tokens = queries.shape[0]
    total_keys = keys_values.shape[0]
    chunk = min(total_keys, 512)
    scale = HD ** (-0.5)
    for g in range(KV):
        query = side_by_side(queries[...], g * group_size, group_size)
        incoming = side_by_side(mixed_grad[...], g * group_size, group_size)
        rows = []
        for h in range(group_size):
            spot = slice((g * group_size + h) * HD, (g * group_size + h + 1) * HD)
            product = mixed_grad[:, spot].astype(jnp.float32) * mixed[:, spot]
            rows.append(jnp.sum(product.T, axis=0, keepdims=True))
        row_dot = jnp.concatenate(rows, axis=1)
        turned_grad = jnp.zeros((HD, group_size * tokens), jnp.float32)
        for start in range(0, total_keys, chunk):
            part = slice(start, start + chunk)
            keys = keys_values[part, g * HD : (g + 1) * HD]
            values = keys_values[part, (KV + g) * HD : (KV + g + 1) * HD]
            scores = dot_nt(keys, query) * scale
            scores = scores + jnp.concatenate([hidden_by[part, :]] * group_size, axis=1)
            probs = jnp.exp(scores - log_total[g : g + 1, :])
            score_grad = (probs * (dot_nt(values, incoming) - row_dot)).astype(low)
            kv_grad[part, g * HD : (g + 1) * HD] = (dot_nn(score_grad, query) * scale).astype(low)
            kv_grad[part, (KV + g) * HD : (KV + g + 1) * HD] = dot_nn(
                probs.astype(low), incoming
            ).astype(low)
            turned_grad += dot_tn(keys, score_grad)
        for h in range(group_size):
            spot = slice((g * group_size + h) * HD, (g * group_size + h + 1) * HD)
            query_grad[:, spot] = turned_grad[:, h * tokens : (h + 1) * tokens].T * scale


def attend_back(queries, keys_values, hidden_by, mixed, log_total, mixed_grad):
    tokens, width = queries.shape
    pairs = keys_values.shape[0] * H * tokens
    return pl.pallas_call(
        attend_back_kernel,
        out_shape=[
            jax.ShapeDtypeStruct((tokens, width), jnp.float32),
            jax.ShapeDtypeStruct(keys_values.shape, low),
        ],
        compiler_params=pltpu.CompilerParams(vmem_limit_bytes=50 * 1024 * 1024),
        cost_estimate=pl.CostEstimate(
            flops=10 * pairs * HD, bytes_accessed=4 * keys_values.size, transcendentals=pairs
        ),
    )(queries, keys_values, hidden_by, mixed, log_total, mixed_grad)


def ff_tile(tokens, cots, gate, up, down):
    gate_pre = dot_nn(tokens, gate)
    up_pre = dot_nn(tokens, up)
    hidden_grad = dot_nt(cots, down)
    sigmoid_gate = jax.nn.sigmoid(gate_pre)
    gate_act = gate_pre * sigmoid_gate
    hidden = (gate_act * up_pre).astype(low)
    gate_grad = hidden_grad * up_pre * sigmoid_gate * (1.0 + gate_pre * (1.0 - sigmoid_gate))
    return hidden, gate_grad.astype(low), (hidden_grad * gate_act).astype(low)


def of_matrix(parts, which):
    return jnp.concatenate([p[:, which].reshape(-1, p.shape[-1]) for p in parts], axis=0)


def ff_kernel(tokens, cots, w0, w1, w2, w3, down, token_grad, out, d0, d1, d2, d3, down_grad, token_total, out_total):
    step = pl.program_id(0)
    weights = [w[...] for w in (w0, w1, w2, w3)]
    gate, up = of_matrix(weights, 0), of_matrix(weights, 1)
    hidden, gate_grad, up_grad = ff_tile(tokens[...], cots[...], gate, up, down[...])

    @pl.when(step == 0)
    def _():
        token_total[...] = jnp.zeros_like(token_total)
        out_total[...] = jnp.zeros_like(out_total)

    token_total[...] += dot_nt(gate_grad, gate) + dot_nt(up_grad, up)
    out_total[...] += dot_nn(hidden, down[...])
    for which, grad in ((0, gate_grad), (1, up_grad)):
        full = dot_tn(tokens[...], grad).astype(low)
        start = 0
        for d in (d0, d1, d2, d3):
            rows = d.shape[0] * d.shape[2]
            d[:, which] = full[start : start + rows].reshape(d.shape[0], d.shape[2], d.shape[3])
            start += rows
    down_grad[...] = dot_tn(hidden, cots[...]).astype(low)

    @pl.when(step == pl.num_programs(0) - 1)
    def _():
        token_grad[...] = token_total[...].astype(low)
        out[...] = out_total[...].astype(low)


def feed_forward(tokens, cots, weights, down):
    count, width = tokens.shape
    columns = down.shape[0]
    tile = 256
    if count > 1024 or columns % tile:
        gate, up = of_matrix(weights, 0), of_matrix(weights, 1)
        hidden, gate_grad, up_grad = ff_tile(tokens, cots, gate, up, down)
        grads = [dot_tn(tokens, g).astype(low) for g in (gate_grad, up_grad)]
        parts = []
        start = 0
        for w in weights:
            rows = w.shape[0] * w.shape[2]
            pair = [g[start : start + rows].reshape(w.shape[0], 1, *w.shape[2:]) for g in grads]
            parts.append(jnp.concatenate(pair, axis=1))
            start += rows
        return (
            (dot_nt(gate_grad, gate) + dot_nt(up_grad, up)).astype(low),
            dot_nn(hidden, down).astype(low),
            *parts,
            dot_tn(hidden, cots).astype(low),
        )
    whole = pl.BlockSpec((count, width), lambda i: (0, 0))
    pieces, _, rows, _ = weights[0].shape
    by_columns = pl.BlockSpec((pieces, 2, rows, tile), lambda i: (0, 0, 0, i))
    by_rows = pl.BlockSpec((tile, width), lambda i: (i, 0))
    wide = jax.ShapeDtypeStruct((count, width), low)
    long = jax.ShapeDtypeStruct(weights[0].shape, low)
    return pl.pallas_call(
        ff_kernel,
        grid=(columns // tile,),
        in_specs=[whole, whole] + [by_columns] * 4 + [by_rows],
        out_specs=[whole, whole] + [by_columns] * 4 + [by_rows],
        out_shape=[wide, wide] + [long] * 4 + [jax.ShapeDtypeStruct((columns, width), low)],
        scratch_shapes=[pltpu.VMEM((count, width), jnp.float32)] * 2,
        compiler_params=pltpu.CompilerParams(
            dimension_semantics=("arbitrary",), vmem_limit_bytes=50 * 1024 * 1024
        ),
        cost_estimate=pl.CostEstimate(
            flops=18 * count * width * columns,
            bytes_accessed=12 * width * columns + 12 * count * width,
            transcendentals=count * columns,
        ),
    )(tokens, cots, *weights, down)


class Grid:
    def __init__(self, size):
        self.size = size
        self.axes = axes_of(size)
        self.rank = len(self.axes)
        self.strides = []
        step = size
        for extent in self.axes:
            step //= extent
            self.strides.append(step)
        index = lax.axis_index("ctx")
        self.place = [(index // s) % e for s, e in zip(self.strides, self.axes)]

    def hop(self, values, moves):
        pairs = []
        for i in range(self.size):
            to = i
            for axis, by in moves.items():
                digit = (i // self.strides[axis]) % self.axes[axis]
                to += (((digit + by) % self.axes[axis]) - digit) * self.strides[axis]
            pairs.append((i, to))
        return lax.ppermute(values, "ctx", pairs)

    def offsets(self, axes):
        return list(itertools.product(*[range(self.axes[a]) for a in axes]))

    def gather_stage(self, values, axes):
        pieces = {}
        for offs in self.offsets(axes):
            pieces[offs] = self.hop(values, dict(zip(axes, offs))) if any(offs) else values

        def join(prefix):
            depth = len(prefix)
            if depth == len(axes):
                return pieces[prefix]
            return jnp.concatenate(
                [join(prefix + (j,)) for j in range(self.axes[axes[depth]])], axis=axes[depth]
            )

        return join(())

    def scatter_stage(self, values, axes, absolute):
        def take(offs):
            part = values
            for axis, back in zip(axes, offs):
                if absolute:
                    spot = (self.place[axis] - back + self.axes[axis]) % self.axes[axis]
                    part = lax.dynamic_slice_in_dim(part, spot, 1, axis=axis)
                else:
                    part = lax.slice_in_dim(part, back, back + 1, axis=axis)
            return part

        total = None
        arrived = []
        for offs in self.offsets(axes):
            part = take(offs)
            if any(offs):
                part = self.hop(part, {a: -o for a, o in zip(axes, offs)})
            arrived.append(part)
        total = arrived[0].astype(jnp.float32)
        for part in arrived[1:]:
            total = total + part.astype(jnp.float32)
        return total.astype(values.dtype)

    def gather(self, parts, orders):
        for stage in range(len(orders[0])):
            (parts,) = together(parts)
            parts = [self.gather_stage(p, o[stage]) for p, o in zip(parts, orders)]
        return parts

    def scatter_round(self, parts, orders, stage, absolute):
        return [
            self.scatter_stage(p, o[len(o) - 1 - stage], absolute) for p, o in zip(parts, orders)
        ]

    def ordered(self, values, axis):
        extent = self.axes[axis]
        wheel = [lax.slice_in_dim(values, j, j + 1, axis=axis) for j in range(extent)]
        wheel = jnp.concatenate(wheel[::-1] + wheel[:0:-1], axis=axis)
        return lax.dynamic_slice_in_dim(wheel, extent - 1 - self.place[axis], extent, axis=axis)

    def source_rows(self, first, count, over):
        index = jnp.int32(0)
        for axis in range(self.rank):
            if axis in over:
                back = jnp.arange(self.axes[axis], dtype=jnp.int32)
            else:
                back = jnp.zeros((1,), jnp.int32)
            digit = (self.place[axis] - back + self.axes[axis]) % self.axes[axis]
            shape = [1] * self.rank
            shape[axis] = digit.shape[0]
            index = index + digit.reshape(shape) * self.strides[axis]
        return index[..., None], first + jnp.arange(count, dtype=jnp.int32)


def together(*groups):
    flat = [v for g in groups for v in (g if isinstance(g, list) else [g])]
    flat = list(lax.optimization_barrier(tuple(flat)))
    out = []
    for g in groups:
        if isinstance(g, list):
            out.append([flat.pop(0) for _ in g])
        else:
            out.append(flat.pop(0))
    return out


def other_core(values):
    return lax.ppermute(values, "fsdp", [(0, 1), (1, 0)])


def both_cores(values, core, axis):
    other = other_core(values)
    first = jnp.where(core == 0, values, other)
    second = jnp.where(core == 0, other, values)
    return jnp.concatenate([first, second], axis=axis)


def own_core_sum(values, core, axis):
    mine = lax.dynamic_slice_in_dim(values, core, 1, axis=axis)
    theirs = lax.dynamic_slice_in_dim(values, 1 - core, 1, axis=axis)
    return mine + other_core(theirs)


def shards(
    tokens_in,
    deal_table,
    cont_id,
    position,
    qkv_weight,
    qkv_bias,
    out_weight,
    attn_gain,
    mlp_gain,
    gate_weight,
    up_weight,
    down_weight,
    cotangent,
):
    ctx_size = lax.axis_size("ctx")
    devices = 2 * ctx_size
    core = lax.axis_index("fsdp")
    grid = Grid(ctx_size)
    all_axes = tuple(range(grid.rank))
    tok_dev, width = tokens_in.shape[1], tokens_in.shape[2]
    block_len = tok_dev // BLOCKS_DEV
    prompt_len = tok_dev * ctx_size // 2
    width_q = H * HD
    width_kv = KV * HD
    deal_row = deal_table[0]
    query_seq = cont_id[0]
    query_pos = position[0]
    hidden_in = tokens_in[0].astype(jnp.float32)
    rows_w = qkv_weight.shape[0]

    ff_axes = (0,) if grid.rank == 3 else all_axes
    far_axes = tuple(a for a in all_axes if a not in ff_axes)
    ff_size = 1
    for a in ff_axes:
        ff_size *= grid.axes[a]
    far_size = ctx_size // ff_size
    ff_total = gate_weight.shape[1]
    ff_cols = ff_total // ff_size
    ff_room = -(-ff_cols // 256) * 256
    members = {}
    for i in range(ctx_size):
        key = tuple((i // grid.strides[a]) % grid.axes[a] for a in far_axes)
        members.setdefault(key, []).append(i)
    groups = [members[k] for k in sorted(members)]

    if grid.rank == 3:
        wide_orders = [((0,), (1, 2))]
        ff_orders = [((0,),)]
        far_orders = [((1,), (2,)), ((2,), (1,))]
    else:
        wide_orders = [tuple((a,) for a in all_axes)]
        ff_orders = wide_orders[:1]
        far_orders = [(), ()]
    weight_order = wide_orders[:1]
    token_bounds = [0, tok_dev]
    ff_bounds = [0, tok_dev]
    far_shape = tuple(grid.axes[a] for a in far_axes)
    spots = ((core - jnp.arange(2, dtype=jnp.int32)) % 2) * rows_w
    spots = spots.reshape((2,) + (1,) * (len(far_axes) + 3))
    for slot, a in enumerate(far_axes):
        digit = (grid.place[a] - jnp.arange(grid.axes[a], dtype=jnp.int32)) % grid.axes[a]
        shape = [1] * (len(far_axes) + 4)
        shape[slot + 2] = grid.axes[a]
        spots = spots + digit.reshape(shape) * (grid.strides[a] * 2 * rows_w)
    steps = [0]
    for a in ff_axes:
        steps = [s + d * grid.strides[a] * 2 * rows_w for s in steps for d in range(grid.axes[a])]
    steps = jnp.array(steps, jnp.int32).reshape((1, 2) + (1,) * len(far_axes) + (ff_size // 2, 1))
    spots = (spots + steps + jnp.arange(rows_w, dtype=jnp.int32)).reshape(-1)
    arrival = (jnp.arange(width, dtype=jnp.int32)[:, None] == spots[None, :]).astype(low)

    def gather_tokens(values, bounds, orders):
        parts = [values[a:b] for a, b in zip(bounds[:-1], bounds[1:])]
        parts = [p.reshape((1,) * grid.rank + p.shape) for p in parts]
        parts = grid.gather(parts, orders)
        return jnp.concatenate([p.reshape(-1, p.shape[-1]) for p in parts], axis=0)

    def cut_tokens(values, bounds, over):
        parts = []
        start = 0
        lead = tuple(grid.axes[a] if a in over else 1 for a in all_axes)
        count = 1
        for e in lead:
            count *= e
        for a, b in zip(bounds[:-1], bounds[1:]):
            rows = count * (b - a)
            parts.append(values[start : start + rows].reshape(lead + (b - a, values.shape[-1])))
            start += rows
        return parts

    def join_tokens(parts):
        return jnp.concatenate([p.reshape(p.shape[grid.rank :]) for p in parts], axis=0)

    def cut_columns(grad, bounds):
        lead = grid.axes + (2, rows_w)
        return [
            own_core_sum(grad[:, a:b].astype(low).reshape(lead + (b - a,)), core, grid.rank)
            for a, b in zip(bounds[:-1], bounds[1:])
        ]

    def join_columns(parts):
        parts = [p.reshape(rows_w, p.shape[-1]) for p in parts]
        return jnp.concatenate(parts, axis=1).astype(jnp.float32)

    stages = len(wide_orders[0])
    ff_stages = len(ff_orders[0])

    bias_len = qkv_bias.shape[0]
    side_len = -(-(2 * rows_w + bias_len) // 128) * 128
    side_rows = jnp.concatenate([attn_gain, mlp_gain, qkv_bias])
    side_rows = jnp.pad(side_rows[None], ((0, rows_w - 1), (0, side_len - side_rows.shape[0])))
    gathered = lax.all_gather(
        jnp.concatenate([qkv_weight, side_rows], axis=1), ("ctx", "fsdp"), axis=0, tiled=True
    )
    def to_columns(weight):
        weight = jnp.swapaxes(weight.reshape(rows_w, ff_size, ff_cols), 0, 1)
        return jnp.pad(weight, ((0, 0), (0, 0), (0, ff_room - ff_cols)))

    gate_up = jnp.stack([to_columns(gate_weight), to_columns(up_weight)], axis=1)
    ones = (1,) * grid.rank
    rows_d = down_weight.shape[0]
    half = width // 2
    down_parts = [down_weight[:, :half].reshape(ones + (rows_d, half))]
    down_parts.append(down_weight[:, half:].reshape(ones + (rows_d, half)))
    out_low = cotangent[0]
    cot_all = gather_tokens(out_low, ff_bounds, ff_orders)

    def gather_far(parts, stage):
        if stage < len(far_orders[0]):
            parts = [grid.gather_stage(p, o[stage]) for p, o in zip(parts, far_orders)]
        return parts

    def scatter_far(parts, stage, absolute):
        if stage < len(far_orders[0]):
            parts = grid.scatter_round(parts, far_orders, stage, absolute)
        return parts

    down_parts = gather_far(down_parts, 0)
    cot_all, down_parts = together(cot_all, down_parts)
    down_parts = gather_far(down_parts, 1)
    for a in far_axes:
        down_parts = [grid.ordered(p, a) for p in down_parts]
    down = jnp.concatenate([p[..., None, :, :] for p in down_parts], axis=-1)
    down = both_cores(down, core, grid.rank).reshape(ff_cols, width)
    down = jnp.pad(down, ((0, ff_room - ff_cols), (0, 0)))
    gathered, out_weight, gate_up, cot_all, down = together(
        gathered, out_weight, gate_up, cot_all, down
    )
    full_out = lax.all_gather(out_weight, ("ctx", "fsdp"), axis=0, tiled=True)

    full_qkv = gathered[:, : width_q + 2 * width_kv]
    side = gathered[:, width_q + 2 * width_kv :].reshape(devices, rows_w, side_len)[:, 0]
    side = side.astype(jnp.float32)
    full_attn_gain = side[:, :rows_w].reshape(-1)
    full_mlp_gain = side[:, rows_w : 2 * rows_w].reshape(-1)
    full_bias = side[:, 2 * rows_w : 2 * rows_w + bias_len].reshape(-1)

    normed = (rms_scale(hidden_in) * full_attn_gain).astype(low)
    projected = jnp.dot(normed, full_qkv, preferred_element_type=jnp.float32) + full_bias
    cosine, sine_table = rope_tables(query_pos)
    query_low = apply_rope(
        projected[:, :width_q].reshape(tok_dev, H, HD), cosine, sine_table
    ).astype(low)
    key_low = apply_rope(
        projected[:, width_q : width_q + width_kv].reshape(tok_dev, KV, HD), cosine, sine_table
    ).astype(low)
    value_low = projected[:, width_q + width_kv :].astype(low)
    query_low = query_low.reshape(tok_dev, width_q)

    kv_all = jnp.concatenate([key_low.reshape(tok_dev, width_kv), value_low], axis=1)
    kv_all = grid.gather_stage(kv_all.reshape(ones + kv_all.shape), wide_orders[0][0])
    kv_all, gate_up = together(kv_all, gate_up)
    gate_up = lax.all_to_all(
        gate_up, "ctx", split_axis=0, concat_axis=0, tiled=True, axis_index_groups=groups
    )
    for stage in range(1, len(wide_orders[0])):
        kv_all = grid.gather_stage(kv_all, wide_orders[0][stage])
    kv_all = kv_all.reshape(-1, 2 * width_kv)
    row_ids = []
    for a, b in zip(token_bounds[:-1], token_bounds[1:]):
        chips, rows = grid.source_rows(a, b - a, all_axes)
        row_ids.append((chips * tok_dev + rows).reshape(-1))
    row_ids = jnp.concatenate(row_ids)
    key_seq, key_pos = key_meta(deal_row, row_ids, block_len, prompt_len)
    allowed = visible_pairs(query_seq, query_pos, key_seq, key_pos).T
    hidden_by = jnp.where(allowed, 0.0, neg_large).astype(jnp.float32)
    mixed, attended, log_total = attend(query_low, kv_all, hidden_by)
    attended, gate_up = together(attended, gate_up)
    few = ff_size // 2
    far_parts = [gate_up[:few], gate_up[few:]]
    far_parts = gather_far([p.reshape(ones + p.shape) for p in far_parts], 0)
    resid = hidden_in + jnp.dot(attended, full_out, preferred_element_type=jnp.float32)
    normed_mlp = (rms_scale(resid) * full_mlp_gain).astype(low)

    arranged = jnp.dot(normed_mlp, arrival, preferred_element_type=jnp.float32).astype(low)
    arranged, far_parts = together(arranged, far_parts)
    mlp_all = gather_tokens(arranged, ff_bounds, ff_orders)
    far_parts = gather_far(far_parts, 1)
    mlp_all, far_parts = together(mlp_all, far_parts)
    far_parts = [p.reshape((-1,) + p.shape[-3:]) for p in far_parts]
    far_parts = far_parts + [other_core(p) for p in far_parts]

    out_grad = out_low.astype(jnp.float32)
    mlp_partial, out_partial, *far_grads, down_grad = feed_forward(
        mlp_all, cot_all, far_parts, down
    )
    far_lead = tuple(grid.axes[a] if a in far_axes else 1 for a in all_axes)
    far_grads = [
        (ours.astype(jnp.float32) + other_core(theirs).astype(jnp.float32)).astype(low)
        for ours, theirs in zip(far_grads[:2], far_grads[2:])
    ]
    far_grads = [g.reshape(far_lead + (few,) + g.shape[1:]) for g in far_grads]
    lead = tuple(grid.axes[a] if a in ff_axes else 1 for a in all_axes)
    out_partial = out_partial.reshape(lead + (tok_dev, width))
    for a in ff_axes:
        out_partial = grid.ordered(out_partial, a)
    down_grad = down_grad[:ff_cols].reshape(far_lead + (2, rows_d, width))
    down_grad = own_core_sum(down_grad, core, grid.rank)
    down_grads = [down_grad[..., :half], down_grad[..., half:]]
    mlp_partial, far_grads = together(mlp_partial, far_grads)
    mlp_parts = cut_tokens(mlp_partial, ff_bounds, ff_axes)
    for stage in range(ff_stages):
        mlp_parts = grid.scatter_round(mlp_parts, ff_orders, stage, False)
    far_grads = scatter_far(far_grads, 0, False)
    mlp_parts, far_grads, out_partial, down_grads = together(
        mlp_parts, far_grads, out_partial, down_grads
    )
    out_sum = lax.psum_scatter(
        out_partial.reshape(-1, width),
        "ctx",
        scatter_dimension=0,
        tiled=True,
        axis_index_groups=groups,
    )
    mlp_normed_grad = jnp.einsum(
        "tc,dc->td", join_tokens(mlp_parts), arrival, preferred_element_type=jnp.float32
    )
    resid_part, mlp_gain_grad = norm_back(resid, full_mlp_gain, mlp_normed_grad)
    resid_grad = out_grad + resid_part
    resid_low = resid_grad.astype(low)
    out_w_grad = jnp.einsum("tq,td->qd", attended, resid_low, preferred_element_type=jnp.float32)
    out_w_grad, resid_low = together(out_w_grad.astype(low), resid_low)
    out_w_sum = own_core_sum(out_w_grad.reshape(ctx_size, 2, rows_w, width), core, 1)
    mixed_grad = jnp.einsum(
        "td,qd->tq", resid_low, full_out, preferred_element_type=jnp.float32
    ).astype(low)
    query_rot, kv_partial = attend_back(
        query_low, kv_all, hidden_by, mixed, log_total, mixed_grad
    )
    kv_partial, query_rot, out_w_sum = together(kv_partial, query_rot, out_w_sum)
    out_w_sum = lax.psum_scatter(
        out_w_sum.reshape(ctx_size * rows_w, width),
        "ctx",
        scatter_dimension=0,
        tiled=True,
        axis_index_groups=groups,
    )
    query_grad = rope_back(query_rot.reshape(tok_dev, H, HD), cosine, sine_table)
    query_grad = query_grad.reshape(tok_dev, width_q)
    query_parts = cut_columns(
        jnp.einsum("td,tc->dc", normed, query_grad.astype(low), preferred_element_type=jnp.float32),
        (0, width_q),
    )

    kv_parts = cut_tokens(kv_partial, token_bounds, all_axes)
    kv_parts = grid.scatter_round(kv_parts, wide_orders, 0, False)
    kv_parts, far_grads, query_parts, down_grads = together(
        kv_parts, far_grads, query_parts, down_grads
    )
    for stage in range(1, stages):
        kv_parts = grid.scatter_round(kv_parts, wide_orders, stage, False)
    far_grads = scatter_far(far_grads, 1, False)
    kv_share = join_tokens(kv_parts).astype(jnp.float32)
    kv_share, query_parts, far_grads, down_grads = together(
        kv_share, query_parts, far_grads, down_grads
    )
    gate_up_grad = jnp.concatenate([g.reshape((few,) + g.shape[-3:]) for g in far_grads], axis=0)
    gate_up_grad = lax.all_to_all(
        gate_up_grad, "ctx", split_axis=0, concat_axis=0, tiled=True, axis_index_groups=groups
    )
    query_parts = grid.scatter_round(query_parts, weight_order, 0, True)
    down_grads = scatter_far(down_grads, 0, True)
    key_grad_own = rope_back(
        kv_share[:, :width_kv].reshape(tok_dev, KV, HD), cosine, sine_table
    )
    kv_grad = jnp.concatenate(
        [key_grad_own.reshape(tok_dev, width_kv), kv_share[:, width_kv:]], axis=1
    )
    proj_grad = jnp.concatenate([query_grad, kv_grad], axis=1)
    bias_grad = jnp.sum(proj_grad, axis=0)
    proj_low = proj_grad.astype(low)
    normed_grad = jnp.einsum("tc,dc->td", proj_low, full_qkv, preferred_element_type=jnp.float32)
    input_part, attn_gain_grad = norm_back(hidden_in, full_attn_gain, normed_grad)
    input_grad = resid_grad + input_part

    input_grad, out_sum = together(input_grad, out_sum)
    layer_out = resid + out_sum.astype(jnp.float32)

    def to_rows(grad):
        return jnp.swapaxes(grad, 0, 1).reshape(rows_w, ff_total)

    small = [
        bias_grad[: width_q + width_kv],
        bias_grad[width_q + width_kv :],
        attn_gain_grad,
        mlp_gain_grad,
    ]
    small = jnp.concatenate([v.reshape(devices, 1, -1) for v in small], axis=2).astype(low)
    sizes = ((width_q + width_kv) // devices, width_kv // devices, rows_w, rows_w)
    small = jnp.pad(small, ((0, 0), (0, rows_w - 1), (0, -small.shape[2] % 128)))
    kv_w_grad = jnp.einsum(
        "td,tc->dc", normed, kv_grad.astype(low), preferred_element_type=jnp.float32
    ).astype(low)
    kv_w_grad = jnp.concatenate([kv_w_grad, small.reshape(width, -1)], axis=1)
    kv_w_parts = cut_columns(kv_w_grad, (0, kv_w_grad.shape[1]))
    if far_axes:
        out_w_sum = out_w_sum.reshape(far_lead + (rows_w, width))
        out_w_sum = grid.scatter_stage(out_w_sum, far_axes, True)
    query_parts, kv_w_parts, down_grads, out_w_sum, gate_up_grad = together(
        query_parts, kv_w_parts, down_grads, out_w_sum, gate_up_grad
    )
    out_share = out_w_sum.reshape(rows_w, width).astype(jnp.float32)
    down_grads = scatter_far(down_grads, 1, True)
    down_grad = jnp.concatenate(down_grads, axis=-1)
    down_share = down_grad.reshape(rows_d, width).astype(jnp.float32)
    for stage in range(1, stages):
        query_parts = grid.scatter_round(query_parts, weight_order, stage, True)
    for stage in range(stages):
        kv_w_parts = grid.scatter_round(kv_w_parts, weight_order, stage, True)
    kv_w_share = join_columns(kv_w_parts)
    small = kv_w_share[0, 2 * width_kv :]
    qkv_share = jnp.concatenate([join_columns(query_parts), kv_w_share[:, : 2 * width_kv]], axis=1)
    gate_up_grad = gate_up_grad.astype(jnp.float32)
    gate_share = to_rows(gate_up_grad[:, 0, :, :ff_cols])
    up_share = to_rows(gate_up_grad[:, 1, :, :ff_cols])
    vectors = []
    start = 0
    for count in sizes:
        vectors.append(small[start : start + count])
        start += count
    front_share, value_bias_share, attn_gain_share, mlp_gain_share = vectors
    return (
        layer_out.astype(low)[None],
        input_grad[None],
        qkv_share,
        front_share,
        value_bias_share,
        out_share,
        attn_gain_share,
        mlp_gain_share,
        gate_share,
        up_share,
        down_share,
    )


def solution(mesh):
    return jax.shard_map(
        shards,
        mesh=mesh,
        in_specs=(
            P("fsdp", "ctx", None),
            P("fsdp", None),
            P("fsdp", "ctx"),
            P("fsdp", "ctx"),
            P(("ctx", "fsdp"), None),
            P(("ctx", "fsdp")),
            P(("ctx", "fsdp"), None),
            P(("ctx", "fsdp")),
            P(("ctx", "fsdp")),
            P(("ctx", "fsdp"), None),
            P(("ctx", "fsdp"), None),
            P(("ctx", "fsdp"), None),
            P("fsdp", "ctx", None),
        ),
        out_specs=(
            P("fsdp", "ctx", None),
            P("fsdp", "ctx", None),
            P(("ctx", "fsdp"), None),
            P(("ctx", "fsdp")),
            P(("ctx", "fsdp")),
            P(("ctx", "fsdp"), None),
            P(("ctx", "fsdp")),
            P(("ctx", "fsdp")),
            P(("ctx", "fsdp"), None),
            P(("ctx", "fsdp"), None),
            P(("ctx", "fsdp"), None),
        ),
        check_vma=False,
    )
```
